256 devices in a mesh: ctx: 16 (over z_lo, y), ep: 16 (over z_hi, x, core).
Axes of the slice: x: 4, y: 4, z: 8 (z_hi: 2, z_lo: 4; z = z_hi * 4 + z_lo), core: 2. Of those that a mesh axis runs over, the one named last changes fastest.
Arguments:
- queries: bfloat16 [4096, 8192], P('ctx', 'ep'), may hold values from -80 to 80
- key_states: bfloat16 [4096, 512], P('ctx'), may hold values from -4 to 4
- value_head_states: bfloat16 [4096, 512], P('ctx'), may hold values from -6 to 6
- block_order: int32 [32], P('ctx'), may hold values from 0 to 31, each once
- out_proj: bfloat16 [8192, 4096], P('ep', 'ctx'), may hold values from -0.0625 to 0.0625
- residual: bfloat16 [4096, 4096], P(('ctx', 'ep')), may hold values from -6 to 6
- norm_gain: float32 [4096], replicated, may hold values from 0.25 to 1.75
- w_gate: bfloat16 [4096, 98304], P(None, ('ctx', 'ep')), may hold values from -0.09375 to 0.09375
- w_up: bfloat16 [4096, 98304], P(None, ('ctx', 'ep')), may hold values from -0.09375 to 0.09375
- w_down: bfloat16 [98304, 4096], P(('ctx', 'ep')), may hold values from -0.21875 to 0.21875
- routes: int32 [4096, 8], P(('ctx', 'ep')), may hold values from 0 to 127, all different within a row; in each aligned block of 16 rows (0 to 15, 16 to 31, ...) at most 3 rows name the same one
- gate_weights: float32 [4096, 8], P(('ctx', 'ep')), may hold values from 0.2 to 0.8
Outputs:
- layer_output: bfloat16 [4096, 4096], P(('ctx', 'ep'))
The draws below stay inside these ranges and needn't reach their ends.
Inputs may be any that keep to these rules, and one draw needn't show every extreme that they name: `block_order`: each number once. `routes`: 8 different experts a row; in the rows of one device no expert is named by more than 3 rows, a bound that some block reaches.
All inputs are finite; a program needn't handle non-finite values.
Results may differ from the reference program's by a relative error of at most 0.02.
Values may be sent and summed in bfloat16 or wider, within the bound.
A program may use at most 128 MiB of HBM per device.

```python
import math
import jax
import jax.numpy as jnp
import numpy as np
from jax import lax

D = 4096
QUERY_HEADS = 64
KEY_HEADS = 4
HEAD_SIZE = 128
FF = 768
TOP = 8
SPLIT = 2
CONTEXT_TOKENS = 256
HALF = 128
BLOCKS = 32
SEQUENCE_TOKENS = 4096
TOK_DEV = 16
QUERY_PER_KEY = 16
EXPERTS = 128
CAP = 3
N_CTX = 16
N_EP = 16


def picked_rows(key):
    base_key = jax.random.fold_in(key, 101)
    row_index = jnp.arange(SEQUENCE_TOKENS, dtype=jnp.int32)
    coin_flip = jax.random.bernoulli(base_key, 0.125, (SEQUENCE_TOKENS,))
    return jnp.logical_and(coin_flip, row_index % 8 == 3).astype(jnp.float32)


def common_key_rows(key, pull_weight):
    random_jitter = jax.random.normal(jax.random.fold_in(key, 102), (SEQUENCE_TOKENS, KEY_HEADS * HEAD_SIZE), jnp.float32)
    drawn_field = jnp.clip(random_jitter, -4.0, 4.0)
    ahead_mask = jnp.roll(picked_rows(key), -1)[:, None] * pull_weight
    return drawn_field * (1.0 - ahead_mask)


def draw_key_states(key, part):
    key_region = common_key_rows(key, 0.0)
    return key_region.astype(jnp.bfloat16)


def draw_queries(key, part):
    own_key = jax.random.fold_in(key, 5)
    random_jitter = jnp.clip(jax.random.normal(own_key, (SEQUENCE_TOKENS, QUERY_HEADS * HEAD_SIZE), jnp.float32), -4.0, 4.0) * 2.0
    return random_jitter.astype(jnp.bfloat16)


def levels(key, shape, cuts, least, largest):
    def one(position, blocks):
        draws = jax.random.uniform(jax.random.fold_in(jax.random.fold_in(key, 6), position), (blocks,), jnp.float32, least / len(cuts), largest / len(cuts))
        return jnp.repeat(jnp.exp(draws), shape[position] // blocks).reshape((-1,) + (1,) * (len(shape) - position - 1))

    factor_of = one(*cuts[0])
    for cut in cuts[1:]:
        factor_of = factor_of * one(*cut)
    return factor_of


def deal_out(stream_key, own, number, rows, number_of, top, bound, skew):
    ranking = jax.random.permutation(stream_key, number_of)
    crowded, ordinary = shares(number_of, rows * top, bound, skew, True), shares(number_of, rows * top, bound, skew, False)
    places = jnp.arange(number_of)

    def named(lengths, turn):
        used = int((lengths > 0).sum())
        fixed = max(1, used // 4)
        shifted = fixed + (places - fixed + turn * (used - fixed)) % max(1, number_of - fixed)
        return jnp.zeros((number_of,), jnp.int32).at[ranking[jnp.where(places < fixed, places, shifted)]].set(jnp.asarray(lengths, jnp.int32))

    lengths = jnp.where(number % 4 == 0, named(crowded, number // 4), named(ordinary, number - number // 4 - 1))
    mixed = jax.random.permutation(jax.random.fold_in(own, 3), number_of)
    source_of, receiver = mixed[0:number_of // 2 * 2:2], mixed[1:number_of // 2 * 2:2]
    room = jnp.minimum(lengths[source_of] - 1, bound - lengths[receiver]) // 2
    room = jnp.where((source_of == ranking[0]) | (receiver == ranking[0]) | (lengths[receiver] == 0), 0, jnp.maximum(room, 0))
    shifted = jax.random.randint(jax.random.fold_in(own, 4), (number_of // 2,), 0, 1 << 20) % (room + 1)
    lengths = lengths.at[source_of].add(-shifted).at[receiver].add(shifted)
    members = jnp.searchsorted(jnp.cumsum(lengths), jnp.arange(rows * top), side="right").astype(jnp.int32)
    listing = members.reshape(top, rows).T
    listing = listing[jax.random.permutation(jax.random.fold_in(own, 1), rows)]
    turn = jax.random.randint(jax.random.fold_in(own, 2), (rows, 1), 0, top)
    return jnp.take_along_axis(listing, (jnp.arange(top)[None, :] + turn) % top, axis=1)


def shares(amount, total, bound, skew, full):
    loads = [(1 << 20) // math.isqrt(grade ** skew) + 1 for grade in range(1, amount + 1)]
    largest = bound if full else min(bound, max(-(-total // amount), total * loads[0] // sum(loads)))
    least = 1 if total - largest >= amount - 1 else 0
    holding, rest = [largest] + [least] * (amount - 1), total - largest - least * (amount - 1)
    while rest > 0:
        movable = [i for i in range(1, amount) if holding[i] < largest] or [i for i in range(1, amount) if holding[i] < bound]
        whole, left = sum([loads[i] for i in movable]), rest
        for i in movable:
            more = min(bound - holding[i], max(1, left * loads[i] // whole), rest)
            holding[i] = holding[i] + more
            rest = rest - more
    return np.array(holding)


def bell_draw(stream_key, dims, deviation, most, pieces=(), kind=jnp.bfloat16):
    entries = jax.random.normal(stream_key, dims, jnp.float32) * deviation
    if len(pieces) > 0:
        entries = levels(stream_key, dims, pieces, -0.22, 0.18) * entries
    return jnp.clip(entries, min=-most, max=most).astype(kind)


def setup_inputs(seed: int = 0) -> dict:
    streams_of = jax.random.split(jax.random.key(seed), 13)
    queries = draw_queries(jax.random.fold_in(streams_of[12], 71), 0)
    key_states = draw_key_states(jax.random.fold_in(streams_of[12], 71), 0)
    value_head_states = bell_draw(streams_of[2], (SEQUENCE_TOKENS, KEY_HEADS * HEAD_SIZE), 1.0, 6.0, ((0, 16),))
    block_order = jax.random.permutation(streams_of[3], BLOCKS).astype(jnp.int32)
    out_proj = bell_draw(streams_of[4], (QUERY_HEADS * HEAD_SIZE, D), (QUERY_HEADS * HEAD_SIZE) ** -0.5, 0.0625, ((0, 16), (1, 16)))
    residual = bell_draw(streams_of[5], (SEQUENCE_TOKENS, D), 1.0, 6.0, ((0, 256),))
    norm_gain = jnp.clip(1.0 + 0.15 * jax.random.normal(streams_of[6], (D,), jnp.float32), 0.25, 1.75)
    w_gate = bell_draw(streams_of[7], (D, EXPERTS * FF), D ** -0.5, 0.09375, ((1, 256),))
    w_up = bell_draw(streams_of[8], (D, EXPERTS * FF), D ** -0.5, 0.09375, ((1, 256),))
    w_down = bell_draw(streams_of[9], (EXPERTS * FF, D), FF ** -0.5, 0.21875, ((0, 256),))
    routes_keys = jax.random.split(jax.random.fold_in(streams_of[10], 1), SEQUENCE_TOKENS // TOK_DEV)
    routes_turns = jax.random.permutation(jax.random.fold_in(streams_of[10], 3), SEQUENCE_TOKENS // TOK_DEV)
    routes = jax.vmap(lambda own, number: deal_out(jax.random.fold_in(streams_of[10], 2), own, number, TOK_DEV, EXPERTS, TOP, CAP, 2))(routes_keys, routes_turns).reshape((SEQUENCE_TOKENS, TOP))
    gate_weights = jnp.clip(0.2 + 0.6 * jax.random.uniform(streams_of[11], (SEQUENCE_TOKENS, TOP), jnp.float32) ** levels(streams_of[11], (SEQUENCE_TOKENS, TOP), ((0, 256),), -0.2, 0.2), 0.2, 0.8)
    return dict(queries=queries, key_states=key_states, value_head_states=value_head_states, block_order=block_order, out_proj=out_proj, residual=residual, norm_gain=norm_gain, w_gate=w_gate, w_up=w_up, w_down=w_down, routes=routes, gate_weights=gate_weights)


NEG_FILL = -1e+30
EPS = 1e-06

def token_positions(block_order):
    offsets = jnp.arange(SEQUENCE_TOKENS, dtype=jnp.int32)
    return block_order[offsets // HALF] * HALF + offsets % HALF

def attention(queries, key_states, value_head_states, positions):
    score_scale = 1.0 / math.sqrt(HEAD_SIZE)
    query_block_list = SEQUENCE_TOKENS // CONTEXT_TOKENS

    def single_entry(item_index):
        head_kv = item_index // query_block_list
        block_index = item_index % query_block_list
        q_rows = lax.dynamic_slice_in_dim(queries, block_index * CONTEXT_TOKENS, CONTEXT_TOKENS, 0)
        q_rows = lax.dynamic_slice_in_dim(q_rows, head_kv * QUERY_PER_KEY * HEAD_SIZE, QUERY_PER_KEY * HEAD_SIZE, 1)
        q_rows = q_rows.reshape(CONTEXT_TOKENS, QUERY_PER_KEY, HEAD_SIZE).astype(jnp.float32)
        k_all = lax.dynamic_slice_in_dim(key_states, head_kv * HEAD_SIZE, HEAD_SIZE, 1).astype(jnp.float32)
        v_all = lax.dynamic_slice_in_dim(value_head_states, head_kv * HEAD_SIZE, HEAD_SIZE, 1).astype(jnp.float32)
        q_pos = lax.dynamic_slice_in_dim(positions, block_index * CONTEXT_TOKENS, CONTEXT_TOKENS, 0)
        allowed = positions[None, :] <= q_pos[:, None]
        scores = jnp.einsum('qhd,kd->hqk', q_rows, k_all) * score_scale
        scores = jnp.where(allowed[None], scores, NEG_FILL)
        row_peak = lax.optimization_barrier(jnp.max(scores, axis=2, keepdims=True))
        weights = jnp.where(allowed[None], jnp.exp(scores - row_peak), 0.0)
        row_total = lax.optimization_barrier(jnp.sum(weights, axis=2))
        rounded = lax.optimization_barrier(weights.astype(jnp.bfloat16)).astype(jnp.float32)
        weighted = jnp.einsum('hqk,kd->hqd', rounded, v_all)
        return (weighted / row_total[:, :, None]).astype(jnp.bfloat16)
    stacked_rows = lax.map(single_entry, jnp.arange(KEY_HEADS * query_block_list, dtype=jnp.int32))
    stacked_rows = stacked_rows.reshape(KEY_HEADS, query_block_list, QUERY_PER_KEY, CONTEXT_TOKENS, HEAD_SIZE).transpose(1, 3, 0, 2, 4)
    return stacked_rows.reshape(SEQUENCE_TOKENS, QUERY_HEADS * HEAD_SIZE)

def projected(attended, out_proj):
    local_heads = QUERY_HEADS // N_EP
    weights = out_proj.reshape(N_EP, local_heads * HEAD_SIZE, D).astype(jnp.float32)

    def one_block(row_block):
        grouped = row_block.reshape(CONTEXT_TOKENS, N_EP, local_heads * HEAD_SIZE).astype(jnp.float32)
        group_part = jnp.einsum('tgk,gkd->tgd', grouped, weights).astype(jnp.bfloat16)
        return lax.optimization_barrier(jnp.sum(lax.optimization_barrier(group_part).astype(jnp.float32), axis=1))
    return lax.map(one_block, attended.reshape(N_CTX, CONTEXT_TOKENS, QUERY_HEADS * HEAD_SIZE)).reshape(SEQUENCE_TOKENS, D)

def experts_out(normed, w_gate, w_up, w_down, routes, gate_weights):
    half_width = FF // SPLIT
    most_rows = N_CTX * N_EP * CAP

    def one_expert(expert_id, running):
        expert_id = expert_id.astype(jnp.int32)
        named_here = routes == expert_id
        chosen = jnp.any(named_here, axis=1)
        weight = lax.optimization_barrier(jnp.sum(jnp.where(named_here, gate_weights, 0.0), axis=1))
        row_count = jnp.sum(chosen.astype(jnp.int32))
        picked = jnp.nonzero(chosen, size=most_rows, fill_value=0)[0].astype(jnp.int32)
        is_valid = jnp.arange(most_rows, dtype=jnp.int32) < row_count
        inputs = normed[picked]
        result = jnp.zeros((most_rows, D), jnp.float32)
        for half_index in range(SPLIT):
            first_col = expert_id * FF + half_index * half_width
            gate_cols = lax.dynamic_slice_in_dim(w_gate, first_col, half_width, 1)
            up_cols = lax.dynamic_slice_in_dim(w_up, first_col, half_width, 1)
            down_rows = lax.dynamic_slice_in_dim(w_down, first_col, half_width, 0)
            gate_pre = jnp.dot(inputs, gate_cols, preferred_element_type=jnp.float32)
            upward = jnp.dot(inputs, up_cols, preferred_element_type=jnp.float32)
            hidden_act = (jax.nn.silu(gate_pre) * upward).astype(jnp.bfloat16)
            half_out = jnp.dot(hidden_act, down_rows, preferred_element_type=jnp.float32).astype(jnp.bfloat16)
            result = result + lax.optimization_barrier(half_out).astype(jnp.float32)
        expert_out = lax.optimization_barrier(result.astype(jnp.bfloat16)).astype(jnp.float32)
        scaled = expert_out * jnp.where(is_valid, weight[picked], 0.0)[:, None]
        return running.at[picked].add(scaled)
    return lax.fori_loop(0, EXPERTS, one_expert, jnp.zeros((SEQUENCE_TOKENS, D), jnp.float32))

def reference(queries, key_states, value_head_states, block_order, out_proj, residual, norm_gain, w_gate, w_up, w_down, routes, gate_weights):
    positions = token_positions(block_order)
    attended = attention(queries, key_states, value_head_states, positions)
    hidden_state = (residual.astype(jnp.float32) + projected(attended, out_proj)).astype(jnp.bfloat16)
    widened = lax.optimization_barrier(hidden_state).astype(jnp.float32)
    normed = (widened * lax.rsqrt(lax.optimization_barrier(jnp.mean(widened * widened, axis=1, keepdims=True)) + EPS) * norm_gain).astype(jnp.bfloat16)
    routed = experts_out(normed, w_gate, w_up, w_down, routes, gate_weights)
    return (widened + routed).astype(jnp.bfloat16)
```

```python
import functools
import math

import jax
import jax.numpy as jnp
import numpy as np
from jax import lax
from jax.experimental import pallas as pl
from jax.experimental.pallas import tpu as pltpu
from jax.sharding import PartitionSpec as P

MESH = pl.DeviceIdType.MESH
BF = jnp.bfloat16
F32 = jnp.float32

D = 4096
HEAD = 128
TOP = 8
NEG = -1e30
EPS = 1e-06
SCALE = 1.0 / math.sqrt(HEAD)

NC = 4
CW = D // NC
ROWS = 16
CAP = 3
SLOT = 8 * CAP
FH = 384


def here():
    c = lax.axis_index("ctx")
    e = lax.axis_index("ep")
    return (e // 2) % 4, c % 4, e // 8, c // 4, e % 2


def device(x, y, z_hi, z_lo, core):
    return (z_lo * 4 + y, z_hi * 8 + x * 2 + core)


def remote(src, dst, send, recv, target):
    return pltpu.make_async_remote_copy(
        src_ref=src, dst_ref=dst, send_sem=send, recv_sem=recv, device_id=target, device_id_type=MESH
    )


def attend_kernel(
    q_ref, k_ref, v_ref, order_ref, proj_ref, resid_ref, gain_ref, routes_ref, gates_ref,
    normed_ref, hidden_ref, pick_ref, weigh_ref,
    kv, scores, qpos, peak, att, proj, part, other, send_x, from_x, send_z, from_z, wide,
    load_sem, zs, zr, ys, yr, cs, cr, ps, pr, as_, ar, d1s, d1r, d2s, d2r, d3s, d3r,
):
    x, y, z_hi, z_lo, core = here()
    partner = device(x, y, z_hi, z_lo, 1 - core)

    def along_z(d):
        return device(x, y, z_hi, (z_lo + d) % 4, core)

    def along_y(d):
        return device(x, (y + d) % 4, z_hi, z_lo, core)

    def along_x(d):
        return device((x + d) % 4, y, z_hi, z_lo, core)

    def along_yz(dy, dz):
        return device(x, (y + 4 - dy) % 4, (z_hi + dz) % 2, z_lo, core)

    head_col = pl.multiple_of((z_hi * 2 + x // 2) * HEAD, HEAD)
    loads = [
        pltpu.make_async_copy(k_ref.at[:, pl.ds(head_col, HEAD)], kv.at[0, 0, 0, pl.ds(0, 256), :], load_sem.at[0]),
        pltpu.make_async_copy(v_ref.at[:, pl.ds(head_col, HEAD)], kv.at[1, 0, 0, pl.ds(0, 256), :], load_sem.at[1]),
        pltpu.make_async_copy(proj_ref, proj.at[0], load_sem.at[2]),
    ]
    for c in loads:
        c.start()

    barrier = pltpu.get_barrier_semaphore()
    peers = [partner]
    peers += [along_z(d) for d in (1, 2, 3)] + [along_y(d) for d in (1, 2, 3)] + [along_x(d) for d in (1, 2, 3)]
    peers += [along_yz(dy, 1) for dy in range(4)]
    for p in peers:
        pl.semaphore_signal(barrier, inc=1, device_id=p, device_id_type=MESH)

    first = order_ref[0].astype(F32)
    second = order_ref[1].astype(F32)
    row16 = lax.broadcasted_iota(jnp.int32, (16, HEAD), 0)
    tail = jnp.where(row16 < 8, first, second).astype(BF)
    kv[0, 0, 0, 256:272, :] = tail
    kv[1, 0, 0, 256:272, :] = tail
    row = lax.broadcasted_iota(jnp.int32, (256, HEAD), 0)
    qpos[...] = jnp.where(row < 128, first * 128.0 + row.astype(F32), (second - 1.0) * 128.0 + row.astype(F32))

    loads[0].wait()
    loads[1].wait()
    pl.semaphore_wait(barrier, len(peers))

    z_copies = [remote(kv.at[core, 0, 0], kv.at[core, d, 0], zs.at[d - 1], zr.at[d - 1], along_z(d)) for d in (1, 2, 3)]
    for c in z_copies:
        c.start()

    def y_copy(d, dy):
        i = d * 3 + dy - 1
        return remote(kv.at[core, d, 0], kv.at[core, d, dy], ys.at[i], yr.at[i], along_y(dy))

    def core_copy(d, dy):
        i = d * 4 + dy
        return remote(kv.at[core, d, dy], kv.at[core, d, dy], cs.at[i], cr.at[i], partner)

    def core_arrival(d, dy):
        i = d * 4 + dy
        return remote(kv.at[1 - core, d, dy], kv.at[1 - core, d, dy], cs.at[i], cr.at[i], partner)

    for d in range(4):
        if d > 0:
            z_copies[d - 1].wait_recv()
        for dy in (1, 2, 3):
            y_copy(d, dy).start()
        if d > 0:
            core_copy(d, 0).start()
    loads[2].wait()
    p_copies = [remote(proj.at[0], proj.at[d], ps.at[d - 1], pr.at[d - 1], along_z(d)) for d in (1, 2, 3)]
    for c in p_copies:
        c.start()

    row = lax.broadcasted_iota(jnp.int32, (128, 128), 0)
    lane = lax.broadcasted_iota(jnp.int32, (128, 128), 1)
    z_to = (z_hi * 4 + z_lo + (row >> 4)) & 7
    x_to = (x + ((row >> 2) & 3)) & 3
    y_to = (y + (row & 3)) & 3
    expert = (z_to & 3) * 32 + y_to * 8 + (z_to >> 2) * 4 + x_to
    own = (lane >> 4) == (row >> 4)
    named = jnp.zeros((128, 128), F32)
    weight = jnp.zeros((128, 128), F32)
    for j in range(TOP):
        hit = jnp.where(own & (routes_ref[j : j + 1, :] == expert), 1.0, 0.0)
        named = named + hit
        weight = weight + hit * gates_ref[j : j + 1, :]
    before = jnp.where(row < lane, 1.0, 0.0).astype(BF)
    rank = jnp.dot(named.astype(BF), before, preferred_element_type=F32)
    for r in range(CAP):
        at = jnp.where((named > 0.5) & (jnp.abs(rank - r) < 0.5), 1.0, 0.0)
        pick_ref[:, r] = at.reshape(8, 16, 128).astype(BF)
        weigh_ref[:, r] = (at * weight).reshape(8, 16, 128).astype(BF)

    for d in range(4):
        for dy in (1, 2, 3):
            y_copy(d, dy).wait_recv()
            core_copy(d, dy).start()
    for d in range(4):
        for dy in range(4):
            if d + dy > 0:
                core_arrival(d, dy).wait_recv()

    lanes = lax.broadcasted_iota(jnp.int32, (8, HEAD), 1).astype(F32)

    def one_head(h, _):
        cols = pl.ds(pl.multiple_of(h * HEAD, HEAD), HEAD)
        query = q_ref[:, cols]

        def score(s, top):
            d, dy = s // 4, s % 4
            keys = kv[0, d, dy, 0:256, :]
            ids = kv[0, d, dy, 256:272, :].astype(F32) * 128.0
            got = lax.dot_general(query, keys, (((1,), (1,)), ((), ())), preferred_element_type=F32)
            at_first = (ids[0:8] + lanes)[0:1]
            at_second = (ids[8:16] + lanes)[0:1]
            left = jnp.where(at_first <= qpos[...], got[:, :HEAD], NEG)
            right = jnp.where(at_second <= qpos[...], got[:, HEAD:], NEG)
            scores[s, :, 0:HEAD] = left
            scores[s, :, HEAD:256] = right
            return jnp.maximum(top, jnp.maximum(left, right))

        top = lax.fori_loop(0, 16, score, jnp.full((256, HEAD), NEG, F32))
        peak[...] = jnp.broadcast_to(jnp.max(top, axis=1, keepdims=True), (256, HEAD))

        def gather(s, carried):
            total, acc = carried
            d, dy = s // 4, s % 4
            left = jnp.exp((scores[s, :, 0:HEAD] - peak[...]) * SCALE)
            right = jnp.exp((scores[s, :, HEAD:256] - peak[...]) * SCALE)
            both = jnp.concatenate([left.astype(BF), right.astype(BF)], axis=1)
            acc = acc + jnp.dot(both, kv[1, d, dy, 0:256, :], preferred_element_type=F32)
            return total + (left + right), acc

        zero = jnp.zeros((256, HEAD), F32)
        total, acc = lax.fori_loop(0, 16, gather, (zero, zero))
        att[0, :, cols] = (acc / jnp.sum(total, axis=1, keepdims=True)).astype(BF)
        for dy in (1, 2, 3):
            remote(att.at[0, :, cols], att.at[dy, :, cols], as_.at[dy - 1], ar.at[dy - 1], along_y(dy)).start()
        return 0

    lax.fori_loop(0, 4, one_head, 0)

    for c in p_copies:
        c.wait_recv()

    def att_copy(dy):
        return remote(att.at[0], att.at[dy], as_.at[dy - 1], ar.at[dy - 1], along_y(dy))

    def core_part(dy):
        return remote(part.at[dy, 1 - core], other.at[dy], d1s.at[dy], d1r.at[dy], partner)

    for dy in range(4):
        if dy > 0:
            att_copy(dy).wait_recv()

        def project(d, _):
            got = jnp.dot(att[dy], proj[d], preferred_element_type=F32).astype(BF)
            got = got.reshape(2, 4, 2, ROWS, 256)
            cols = pl.ds(pl.multiple_of(d * 256, 256), 256)
            part[dy, 0, :, :, :, cols] = got[:, :, 0]
            part[dy, 1, :, :, :, cols] = got[:, :, 1]
            return 0

        lax.fori_loop(0, 4, project, 0)
        core_part(dy).start()

    def x_copy(dy, dx):
        i = dy * 3 + dx - 1
        return remote(send_x.at[dy, dx], from_x.at[dy, dx - 1], d2s.at[i], d2r.at[i], along_x(dx))

    for dy in range(4):
        core_part(dy).wait_recv()
        for dx in (1, 2, 3, 0):
            x_to = (x + dx) % 4
            for dz in range(2):
                z_to = (z_hi + dz) % 2
                mine = part[dy, core, z_to, x_to].astype(F32) + other[dy, z_to, x_to].astype(F32)
                send_x[dy, dx, dz] = mine.astype(BF)
            if dx > 0:
                x_copy(dy, dx).start()

    def yz_copy(dy, dz):
        i = dy * 2 + dz
        return remote(send_z.at[dy, dz], from_z.at[dy, dz], d3s.at[i], d3r.at[i], along_yz(dy, dz))

    for dy in range(4):
        for dx in (1, 2, 3):
            x_copy(dy, dx).wait_recv()
        for dz in (1, 0):
            got = send_x[dy, 0, dz].astype(F32) + from_x[dy, 0, dz].astype(F32)
            got = got + (from_x[dy, 1, dz].astype(F32) + from_x[dy, 2, dz].astype(F32))
            if dy + dz > 0:
                send_z[dy, dz] = got.astype(BF)
                yz_copy(dy, dz).start()
            else:
                from_z[0, 0] = got.astype(BF)

    square = jnp.zeros((ROWS, 256), F32)
    for dy in range(4):
        for dz in range(2):
            if dy + dz > 0:
                yz_copy(dy, dz).wait_recv()
        for d in range(4):
            col = (((z_lo + 4 - d) % 4) * 4 + (y + dy) % 4) * 256
            cols = pl.ds(pl.multiple_of(col, 256), 256)
            got = from_z[dy, 0, :, d * 256 : d * 256 + 256].astype(F32) + from_z[dy, 1, :, d * 256 : d * 256 + 256].astype(F32)
            state = (resid_ref[:, cols].astype(F32) + got).astype(BF)
            hidden_ref[:, cols] = state
            state = state.astype(F32)
            wide[:, cols] = state
            square = square + state * state
    mean = jnp.sum(square, axis=1, keepdims=True) * (1.0 / D)
    normed_ref[...] = (wide[...] * lax.rsqrt(mean + EPS) * gain_ref[...]).astype(BF)

    for c in z_copies + p_copies:
        c.wait_send()
    for d in range(4):
        for dy in (1, 2, 3):
            y_copy(d, dy).wait_send()
        for dy in range(4):
            if d + dy > 0:
                core_copy(d, dy).wait_send()
    for dy in range(4):
        if dy > 0:
            att_copy(dy).wait_send()
        core_part(dy).wait_send()
        for dx in (1, 2, 3):
            x_copy(dy, dx).wait_send()
        for dz in range(2):
            if dy + dz > 0:
                yz_copy(dy, dz).wait_send()


def expert_kernel(
    normed_ref, hidden_ref, pick_ref, weigh_ref, perm_ref, wg_ref, wu_ref, wd_ref,
    out_ref,
    wg, wu, wd, pick, weigh, choose, spread, tok, packed, rows, acc_g, acc_u, act, back, ret, summed, from_z,
    lg, lu, ld, gs, gr, us, ur, ws, wr, os_, or_, ts, tr, xs, xr, rs, rr, fs, fr,
):
    x, y, z_hi, z_lo, core = here()
    z = z_hi * 4 + z_lo
    partner = device(x, y, z_hi, z_lo, 1 - core)

    def along_z(d):
        to = (z + d) % 8
        return device(x, y, to // 4, to % 4, core)

    def in_plane(i):
        return device((x + i // 4) % 4, (y + i % 4) % 4, z_hi, z_lo, core)

    def plane_back(i):
        return device((x + 4 - i // 4) % 4, (y + 4 - i % 4) % 4, z_hi, z_lo, core)

    def chunk(j):
        return pl.ds(pl.multiple_of(j * CW, CW), CW)

    own_half = pl.ds(0, FH)
    far_half = pl.ds(FH, FH)

    def local_g(j):
        return pltpu.make_async_copy(wg_ref.at[chunk(j), :], wg.at[chunk(j), own_half], lg.at[j])

    def local_u(j):
        return pltpu.make_async_copy(wu_ref.at[chunk(j), :], wu.at[chunk(j), own_half], lu.at[j])

    def far_g(j):
        return remote(wg_ref.at[chunk(j), :], wg.at[chunk(j), far_half], gs.at[j], gr.at[j], partner)

    def far_u(j):
        return remote(wu_ref.at[chunk(j), :], wu.at[chunk(j), far_half], us.at[j], ur.at[j], partner)

    local_d = pltpu.make_async_copy(wd_ref, wd.at[own_half, :], ld.at[0])
    far_d = remote(wd_ref, wd.at[far_half, :], ws.at[0], wr.at[0], partner)

    barrier = pltpu.get_barrier_semaphore()
    pl.semaphore_signal(barrier, inc=1, device_id=partner, device_id_type=MESH)

    def greet_z(d, _):
        pl.semaphore_signal(barrier, inc=1, device_id=along_z(d), device_id_type=MESH)
        return 0

    def greet_plane(i, _):
        pl.semaphore_signal(barrier, inc=1, device_id=in_plane(i), device_id_type=MESH)
        return 0

    lax.fori_loop(1, 8, greet_z, 0)
    lax.fori_loop(1, 16, greet_plane, 0)

    for j in range(NC):
        tok[j, 0] = normed_ref[:, j * CW : (j + 1) * CW]
    pick[0] = pick_ref[0]
    weigh[0] = weigh_ref[0]

    pl.semaphore_wait(barrier, 23)

    def send_picks(d, _):
        remote(pick_ref.at[d], pick.at[d], os_.at[0], or_.at[0], along_z(d)).start()
        remote(weigh_ref.at[d], weigh.at[d], os_.at[1], or_.at[1], along_z(d)).start()
        return 0

    def all_picks():
        return (
            remote(pick_ref.at[pl.ds(1, 7)], pick.at[pl.ds(1, 7)], os_.at[0], or_.at[0], partner),
            remote(weigh_ref.at[pl.ds(1, 7)], weigh.at[pl.ds(1, 7)], os_.at[1], or_.at[1], partner),
        )

    def send_tokens(j, _):
        def one(d, _):
            remote(tok.at[j, 0], tok.at[j, d], ts.at[j], tr.at[j], along_z(d)).start()
            return 0

        lax.fori_loop(1, 8, one, 0)
        return 0

    lax.fori_loop(1, 8, send_picks, 0)
    lax.fori_loop(0, NC, send_tokens, 0)
    for j in range(NC):
        local_g(j).start()
        local_u(j).start()
        far_g(j).start()
        far_u(j).start()
    local_d.start()
    far_d.start()

    acc_g[...] = jnp.zeros_like(acc_g)
    acc_u[...] = jnp.zeros_like(acc_u)

    for c in all_picks():
        c.wait_recv()
    perm = perm_ref[...]
    choose[...] = jnp.dot(perm, pick[...].reshape(16 * SLOT, 128), preferred_element_type=F32).astype(BF)
    spread[...] = jnp.dot(perm, weigh[...].reshape(16 * SLOT, 128), preferred_element_type=F32).T.astype(BF)

    def all_tokens(j):
        return remote(tok.at[j, pl.ds(1, 7)], tok.at[j, pl.ds(1, 7)], ts.at[j], tr.at[j], partner)

    def all_rows(j):
        return remote(packed.at[j], rows.at[j, pl.ds(1, 15)], xs.at[j], xr.at[j], partner)

    def all_back(j):
        return remote(back.at[j], ret.at[j, pl.ds(1, 15)], rs.at[j], rr.at[j], partner)

    def all_sums(j):
        return remote(summed.at[j, pl.ds(1, 7)], from_z.at[j, pl.ds(1, 7)], fs.at[j], fr.at[j], partner)

    def pack(j, _):
        all_tokens(j).wait_recv()

        def columns(n, _):
            cols = pl.ds(pl.multiple_of(n * 256, 256), 256)
            got = jnp.dot(choose[...], tok[j, :, :, cols].reshape(128, 256), preferred_element_type=F32)
            got = got.astype(BF).reshape(16, SLOT, 256)
            rows[j, 0, :, cols] = got[0]
            packed[j, :, :, cols] = got[1:]
            return 0

        lax.fori_loop(0, CW // 256, columns, 0)

        def send(i, _):
            remote(packed.at[j, i - 1], rows.at[j, i], xs.at[j], xr.at[j], in_plane(i)).start()
            return 0

        lax.fori_loop(1, 16, send, 0)
        return 0

    lax.fori_loop(0, NC, pack, 0)

    def upward(j, _):
        local_g(j).wait()
        local_u(j).wait()
        far_g(j).wait_recv()
        far_u(j).wait_recv()
        all_rows(j).wait_recv()

        def columns(n, _):
            cols = pl.ds(pl.multiple_of(n * 256, 256), 256)
            got = rows[j].reshape(16 * SLOT, CW)
            acc_g[:, cols] += jnp.dot(got, wg[chunk(j), cols], preferred_element_type=F32)
            acc_u[:, cols] += jnp.dot(got, wu[chunk(j), cols], preferred_element_type=F32)
            return 0

        lax.fori_loop(0, 3, columns, 0)
        return 0

    lax.fori_loop(0, NC, upward, 0)
    act[...] = (jax.nn.silu(acc_g[...]) * acc_u[...]).astype(BF)
    local_d.wait()
    far_d.wait_recv()

    def downward(j, _):
        def columns(n, _):
            cols = pl.ds(pl.multiple_of(n * 256, 256), 256)
            far = pl.ds(pl.multiple_of(j * CW + n * 256, 256), 256)
            got = jnp.dot(act[...], wd[:, far], preferred_element_type=F32).astype(BF).reshape(16, SLOT, 256)
            ret[j, 0, :, cols] = got[0]
            back[j, :, :, cols] = got[1:]
            return 0

        lax.fori_loop(0, CW // 256, columns, 0)

        def send(i, _):
            remote(back.at[j, i - 1], ret.at[j, i], rs.at[j], rr.at[j], plane_back(i)).start()
            return 0

        lax.fori_loop(1, 16, send, 0)
        return 0

    lax.fori_loop(0, NC, downward, 0)

    def combine(j, _):
        all_back(j).wait_recv()

        def columns(n, _):
            cols = pl.ds(pl.multiple_of(n * 256, 256), 256)
            got = ret[j, :, :, cols].reshape(16 * SLOT, 256)
            got = jnp.dot(spread[...], got, preferred_element_type=F32)
            summed[j, :, :, cols] = got.astype(BF).reshape(8, ROWS, 256)
            return 0

        lax.fori_loop(0, CW // 256, columns, 0)

        def send(d, _):
            remote(summed.at[j, d], from_z.at[j, d], fs.at[j], fr.at[j], along_z(8 - d)).start()
            return 0

        lax.fori_loop(1, 8, send, 0)
        return 0

    lax.fori_loop(0, NC, combine, 0)

    def finish(j, _):
        all_sums(j).wait_recv()
        total = summed[j, 0].astype(F32)
        for d in range(1, 8):
            total = total + from_z[j, d].astype(F32)
        out_ref[:, chunk(j)] = (hidden_ref[:, chunk(j)].astype(F32) + total).astype(BF)
        return 0

    lax.fori_loop(0, NC, finish, 0)

    for c in all_picks():
        c.wait_send()

    def drain(j, _):
        far_g(j).wait_send()
        far_u(j).wait_send()
        all_tokens(j).wait_send()
        all_rows(j).wait_send()
        all_back(j).wait_send()
        all_sums(j).wait_send()
        return 0

    lax.fori_loop(0, NC, drain, 0)
    far_d.wait_send()


def slot_order():
    perm = np.zeros((16 * SLOT, 16 * SLOT), np.float32)
    for p in range(16):
        for s in range(8):
            for r in range(CAP):
                perm[p * SLOT + s * CAP + r, s * 16 * CAP + r * 16 + p] = 1.0
    return perm


VMEM = pl.BlockSpec(memory_space=pltpu.VMEM)
SMEM = pl.BlockSpec(memory_space=pltpu.SMEM)
ANY = pl.BlockSpec(memory_space=pl.ANY)
SHAPE = jax.ShapeDtypeStruct
DMA = pltpu.SemaphoreType.DMA


def attend(q, k, v, order, proj, resid, gain, routes, gates):
    return pl.pallas_call(
        attend_kernel,
        out_shape=(
            SHAPE((ROWS, D), BF),
            SHAPE((ROWS, D), BF),
            SHAPE((8, CAP, 16, 128), BF),
            SHAPE((8, CAP, 16, 128), BF),
        ),
        in_specs=[VMEM, ANY, ANY, SMEM, ANY, VMEM, VMEM, VMEM, VMEM],
        out_specs=(VMEM,) * 4,
        scratch_shapes=[
            pltpu.VMEM((2, 4, 4, 272, HEAD), BF),
            pltpu.VMEM((16, 256, 256), F32),
            pltpu.VMEM((256, HEAD), F32),
            pltpu.VMEM((256, HEAD), F32),
            pltpu.VMEM((4, 256, 512), BF),
            pltpu.VMEM((4, 512, 256), BF),
            pltpu.VMEM((4, 2, 2, 4, ROWS, 1024), BF),
            pltpu.VMEM((4, 2, 4, ROWS, 1024), BF),
            pltpu.VMEM((4, 4, 2, ROWS, 1024), BF),
            pltpu.VMEM((4, 3, 2, ROWS, 1024), BF),
            pltpu.VMEM((4, 2, ROWS, 1024), BF),
            pltpu.VMEM((4, 2, ROWS, 1024), BF),
            pltpu.VMEM((ROWS, D), F32),
            DMA((3,)),
            DMA((3,)), DMA((3,)),
            DMA((12,)), DMA((12,)),
            DMA((16,)), DMA((16,)),
            DMA((3,)), DMA((3,)),
            DMA((3,)), DMA((3,)),
            DMA((4,)), DMA((4,)),
            DMA((12,)), DMA((12,)),
            DMA((8,)), DMA((8,)),
        ],
        compiler_params=pltpu.CompilerParams(
            collective_id=0, has_side_effects=True, vmem_limit_bytes=48 * 1024 * 1024
        ),
        name="attend",
    )(q, k, v, order, proj, resid, gain, routes, gates)


def route_and_expert(normed, hidden, pick, weigh, perm, wg, wu, wd):
    return pl.pallas_call(
        expert_kernel,
        out_shape=SHAPE((ROWS, D), BF),
        in_specs=[VMEM, VMEM, VMEM, VMEM, VMEM, ANY, ANY, ANY],
        out_specs=VMEM,
        scratch_shapes=[
            pltpu.VMEM((D, 2 * FH), BF),
            pltpu.VMEM((D, 2 * FH), BF),
            pltpu.VMEM((2 * FH, D), BF),
            pltpu.VMEM((8, CAP, 16, 128), BF),
            pltpu.VMEM((8, CAP, 16, 128), BF),
            pltpu.VMEM((16 * SLOT, 128), BF),
            pltpu.VMEM((128, 16 * SLOT), BF),
            pltpu.VMEM((NC, 8, ROWS, CW), BF),
            pltpu.VMEM((NC, 15, SLOT, CW), BF),
            pltpu.VMEM((NC, 16, SLOT, CW), BF),
            pltpu.VMEM((16 * SLOT, 2 * FH), F32),
            pltpu.VMEM((16 * SLOT, 2 * FH), F32),
            pltpu.VMEM((16 * SLOT, 2 * FH), BF),
            pltpu.VMEM((NC, 15, SLOT, CW), BF),
            pltpu.VMEM((NC, 16, SLOT, CW), BF),
            pltpu.VMEM((NC, 8, ROWS, CW), BF),
            pltpu.VMEM((NC, 8, ROWS, CW), BF),
            DMA((NC,)), DMA((NC,)), DMA((1,)),
            DMA((NC,)), DMA((NC,)), DMA((NC,)), DMA((NC,)), DMA((1,)), DMA((1,)),
            DMA((2,)), DMA((2,)),
            DMA((NC,)), DMA((NC,)),
            DMA((NC,)), DMA((NC,)),
            DMA((NC,)), DMA((NC,)),
            DMA((NC,)), DMA((NC,)),
        ],
        compiler_params=pltpu.CompilerParams(
            collective_id=1, has_side_effects=True, vmem_limit_bytes=58 * 1024 * 1024
        ),
        name="experts",
    )(normed, hidden, pick, weigh, perm, wg, wu, wd)


def local(
    queries,
    key_states,
    value_head_states,
    block_order,
    out_proj,
    residual,
    norm_gain,
    w_gate,
    w_up,
    w_down,
    routes,
    gate_weights,
):
    routes_row = jnp.tile(routes.T, (1, 8))
    gates_row = jnp.tile(gate_weights.T, (1, 8))
    normed, hidden, pick, weigh = attend(
        queries, key_states, value_head_states, block_order, out_proj, residual,
        norm_gain.reshape(1, D), routes_row, gates_row,
    )
    perm = jnp.asarray(slot_order(), BF)
    return route_and_expert(normed, hidden, pick, weigh, perm, w_gate, w_up, w_down)


def solution(mesh):
    return jax.shard_map(
        local,
        mesh=mesh,
        in_specs=(
            P("ctx", "ep"),
            P("ctx", None),
            P("ctx", None),
            P("ctx"),
            P("ep", "ctx"),
            P(("ctx", "ep"), None),
            P(),
            P(None, ("ctx", "ep")),
            P(None, ("ctx", "ep")),
            P(("ctx", "ep"), None),
            P(("ctx", "ep"), None),
            P(("ctx", "ep"), None),
        ),
        out_specs=P(("ctx", "ep"), None),
        check_vma=False,
    )
```

```python
import math

import jax
import jax.numpy as jnp
import numpy as np
from jax import lax
from jax.experimental import pallas as pl
from jax.experimental.pallas import tpu as pltpu
from jax.sharding import PartitionSpec as P

MESH = pl.DeviceIdType.MESH
BF = jnp.bfloat16
F32 = jnp.float32

D = 4096
HEAD = 128
TOP = 8
NEG = -1e30
EPS = 1e-06
SCALE = 1.0 / math.sqrt(HEAD)

SUB = 2
NC = 4 * SUB
CW = D // NC
ROWS = 16
CAP = 3
SLOT = 8 * CAP
SLOTS = 16 * SLOT
FH = 384


def here():
    c = lax.axis_index("ctx")
    e = lax.axis_index("ep")
    return (e // 2) % 4, c % 4, e // 8, c // 4, e % 2


def device(x, y, z_hi, z_lo, core):
    return (z_lo * 4 + y, z_hi * 8 + x * 2 + core)


def remote(src, dst, send, recv, target):
    return pltpu.make_async_remote_copy(
        src_ref=src, dst_ref=dst, send_sem=send, recv_sem=recv, device_id=target, device_id_type=MESH
    )


def layer_kernel(
    order_ref, q_hbm, k_hbm, v_hbm, proj_hbm, resid_hbm, gain_hbm, routes_hbm, perm_hbm, wg_hbm, wu_hbm, wd_hbm,
    out_ref,
    query, resid, gain, routing, perm,
    kv, scores, qpos, peak, total, acc, att, proj, part, other, send_x, from_x, send_z, from_z, hidden,
    wg, wu, wd, pick, weigh, pick_in, weigh_in, choose, spread,
    tok, scale, packed, rows, scale_out, scale_in, acc_g, acc_u, act, back, ret, summed, sums_in,
    load_sem, zs, zr, ys, yr, cs, cr, ps, pr, as_, ar, d1s, d1r, d2s, d2r, d3s, d3r,
    lg, lu, ld, gs, gr, us, ur, ws, wr, os_, or_, ts, tr, ss, sr, xs, xr, rs, rr, fs, fr,
):
    x, y, z_hi, z_lo, core = here()
    z = z_hi * 4 + z_lo
    partner = device(x, y, z_hi, z_lo, 1 - core)

    def in_span(d):
        return device(x, y, z_hi, (z_lo + d) % 4, core)

    def along_y(d):
        return device(x, (y + d) % 4, z_hi, z_lo, core)

    def along_x(d):
        return device((x + d) % 4, y, z_hi, z_lo, core)

    def along_yz(dy, dz):
        return device(x, (y + 4 - dy) % 4, (z_hi + dz) % 2, z_lo, core)

    def along_z(d):
        to = (z + d) % 8
        return device(x, y, to // 4, to % 4, core)

    def in_plane(i):
        return device((x + i // 4) % 4, (y + i % 4) % 4, z_hi, z_lo, core)

    def plane_back(i):
        return device((x + 4 - i // 4) % 4, (y + 4 - i % 4) % 4, z_hi, z_lo, core)

    def chunk(c):
        return pl.ds(pl.multiple_of(c * CW, CW), CW)

    def tile(n):
        return pl.ds(pl.multiple_of(n * 256, 256), 256)

    head_col = pl.multiple_of((z_hi * 2 + x // 2) * HEAD, HEAD)
    loads = [
        pltpu.make_async_copy(src, dst, load_sem.at[i])
        for i, (src, dst) in enumerate([
            (k_hbm.at[:, pl.ds(head_col, HEAD)], kv.at[0, 0, 0, pl.ds(0, 256), :]),
            (v_hbm.at[:, pl.ds(head_col, HEAD)], kv.at[1, 0, 0, pl.ds(0, 256), :]),
            (proj_hbm, proj.at[0]),
            (q_hbm, query),
            (routes_hbm, routing),
            (perm_hbm, perm),
            (resid_hbm, resid),
            (gain_hbm, gain),
        ])
    ]
    for c in loads:
        c.start()

    barrier = pltpu.get_barrier_semaphore()

    def greet(target):
        pl.semaphore_signal(barrier, inc=1, device_id=target, device_id_type=MESH)

    def greet_z(d, _):
        greet(along_z(d))
        return 0

    def greet_plane(i, _):
        greet(in_plane(i))
        return 0

    greet(partner)
    lax.fori_loop(1, 8, greet_z, 0)
    lax.fori_loop(1, 16, greet_plane, 0)
    for dy in (1, 2, 3):
        greet(along_yz(dy, 1))

    first = order_ref[0].astype(F32)
    second = order_ref[1].astype(F32)
    row16 = lax.broadcasted_iota(jnp.int32, (16, HEAD), 0)
    tail = jnp.where(row16 < 8, first, second).astype(BF)
    kv[0, 0, 0, 256:272, :] = tail
    kv[1, 0, 0, 256:272, :] = tail
    row = lax.broadcasted_iota(jnp.int32, (256, HEAD), 0)
    qpos[...] = jnp.where(row < 128, first * 128.0 + row.astype(F32), (second - 1.0) * 128.0 + row.astype(F32))

    loads[0].wait()
    loads[1].wait()
    pl.semaphore_wait(barrier, 26)

    def z_copy(d):
        return remote(kv.at[core, 0, 0], kv.at[core, d, 0], zs.at[d - 1], zr.at[d - 1], in_span(d))

    def y_copy(d, dy):
        i = d * 3 + dy - 1
        return remote(kv.at[core, d, 0], kv.at[core, d, dy], ys.at[i], yr.at[i], along_y(dy))

    def core_copy(d, dy):
        i = d * 4 + dy
        return remote(kv.at[core, d, dy], kv.at[core, d, dy], cs.at[i], cr.at[i], partner)

    def core_arrival(d, dy):
        i = d * 4 + dy
        return remote(kv.at[1 - core, d, dy], kv.at[1 - core, d, dy], cs.at[i], cr.at[i], partner)

    def proj_copy(d):
        return remote(proj.at[0], proj.at[d], ps.at[d - 1], pr.at[d - 1], in_span(d))

    for d in (1, 2, 3):
        z_copy(d).start()
    for dy in (1, 2, 3):
        y_copy(0, dy).start()

    loads[4].wait()
    row = lax.broadcasted_iota(jnp.int32, (128, 128), 0)
    lane = lax.broadcasted_iota(jnp.int32, (128, 128), 1)
    z_to = (z + (row >> 4)) & 7
    x_to = (x + ((row >> 2) & 3)) & 3
    y_to = (y + (row & 3)) & 3
    expert = ((z_to & 3) * 32 + y_to * 8 + (z_to >> 2) * 4 + x_to).astype(F32)
    own = (lane >> 4) == (row >> 4)
    named = jnp.zeros((128, 128), F32)
    weight = jnp.zeros((128, 128), F32)
    for j in range(TOP):
        hit = jnp.where(own & (jnp.abs(routing[j : j + 1, :] - expert) < 0.5), 1.0, 0.0)
        named = named + hit
        weight = weight + hit * routing[TOP + j : TOP + j + 1, :]
    before = jnp.where(row < lane, 1.0, 0.0).astype(BF)
    rank = jnp.dot(named.astype(BF), before, preferred_element_type=F32)
    for r in range(CAP):
        at = jnp.where((named > 0.5) & (jnp.abs(rank - r) < 0.5), 1.0, 0.0)
        pick[:, r] = at.reshape(8, 16, 128).astype(BF)
        weigh[:, r] = (at * weight).reshape(8, 16, 128).astype(BF)

    for d in (1, 2, 3):
        z_copy(d).wait_recv()
        for dy in (1, 2, 3):
            y_copy(d, dy).start()
        core_copy(d, 0).start()
    loads[2].wait()
    for d in (1, 2, 3):
        proj_copy(d).start()

    def send_picks(d, _):
        remote(pick.at[d], pick_in.at[d], os_.at[0], or_.at[0], along_z(d)).start()
        remote(weigh.at[d], weigh_in.at[d], os_.at[1], or_.at[1], along_z(d)).start()
        return 0

    lax.fori_loop(1, 8, send_picks, 0)
    pick_in[0] = pick[0]
    weigh_in[0] = weigh[0]

    own_half = pl.ds(0, FH)
    far_half = pl.ds(FH, FH)

    def local_g(c):
        return pltpu.make_async_copy(wg_hbm.at[chunk(c), :], wg.at[chunk(c), own_half], lg.at[c])

    def local_u(c):
        return pltpu.make_async_copy(wu_hbm.at[chunk(c), :], wu.at[chunk(c), own_half], lu.at[c])

    def far_g(c):
        return remote(wg_hbm.at[chunk(c), :], wg.at[chunk(c), far_half], gs.at[c], gr.at[c], partner)

    def far_u(c):
        return remote(wu_hbm.at[chunk(c), :], wu.at[chunk(c), far_half], us.at[c], ur.at[c], partner)

    local_d = pltpu.make_async_copy(wd_hbm, wd.at[own_half, :], ld.at[0])
    far_d = remote(wd_hbm, wd.at[far_half, :], ws.at[0], wr.at[0], partner)

    def start_local(c, _):
        local_g(c).start()
        local_u(c).start()
        return 0

    def start_far(c, _):
        far_g(c).start()
        far_u(c).start()
        return 0

    lanes = lax.broadcasted_iota(jnp.int32, (8, HEAD), 1).astype(F32)
    loads[3].wait()

    def group(d, last):
        for dy in range(4):
            if d + dy > 0:
                core_arrival(d, dy).wait_recv()

        def one_head(h, _):
            cols = pl.ds(pl.multiple_of(h * HEAD, HEAD), HEAD)
            q = query[:, cols]
            top = None
            for dy in range(4):
                ids = kv[0, d, dy, 256:272, :].astype(F32) * 128.0
                got = lax.dot_general(
                    q, kv[0, d, dy, 0:256, :], (((1,), (1,)), ((), ())), preferred_element_type=F32
                )
                left = jnp.where((ids[0:8] + lanes)[0:1] <= qpos[...], got[:, :HEAD], NEG)
                right = jnp.where((ids[8:16] + lanes)[0:1] <= qpos[...], got[:, HEAD:], NEG)
                scores[dy, :, 0:HEAD] = left
                scores[dy, :, HEAD:256] = right
                both = jnp.maximum(left, right)
                top = both if top is None else jnp.maximum(top, both)
            now = jnp.broadcast_to(jnp.max(top, axis=1, keepdims=True), (256, HEAD))
            if d > 0:
                old = peak[h]
                now = jnp.maximum(now, old)
                shrink = jnp.exp((old - now) * SCALE)
                sums = total[h] * shrink
                out = acc[h] * shrink
            else:
                sums = jnp.zeros((256, HEAD), F32)
                out = jnp.zeros((256, HEAD), F32)
            peak[h] = now
            for dy in range(4):
                left = jnp.exp((scores[dy, :, 0:HEAD] - peak[h]) * SCALE)
                right = jnp.exp((scores[dy, :, HEAD:256] - peak[h]) * SCALE)
                both = jnp.concatenate([left.astype(BF), right.astype(BF)], axis=1)
                out = out + jnp.dot(both, kv[1, d, dy, 0:256, :], preferred_element_type=F32)
                sums = sums + (left + right)
            if last:
                att[0, :, cols] = (out / jnp.sum(sums, axis=1, keepdims=True)).astype(BF)
                for dy in (1, 2, 3):
                    remote(att.at[0, :, cols], att.at[dy, :, cols], as_.at[dy - 1], ar.at[dy - 1], along_y(dy)).start()
            else:
                total[h] = sums
                acc[h] = out
            return 0

        lax.fori_loop(0, 4, one_head, 0)

    for d in range(4):
        for dy in (1, 2, 3):
            y_copy(d, dy).wait_recv()
            core_copy(d, dy).start()
        if d == 0:
            lax.fori_loop(0, NC, start_local, 0)
            local_d.start()
        else:
            group(d - 1, False)
    group(3, True)

    def all_picks():
        return (
            remote(pick.at[pl.ds(1, 7)], pick_in.at[pl.ds(1, 7)], os_.at[0], or_.at[0], partner),
            remote(weigh.at[pl.ds(1, 7)], weigh_in.at[pl.ds(1, 7)], os_.at[1], or_.at[1], partner),
        )

    for c in all_picks():
        c.wait_recv()
    loads[5].wait()
    choose[...] = jnp.dot(perm[...], pick_in[...].reshape(SLOTS, 128), preferred_element_type=F32).astype(BF)
    spread[...] = jnp.dot(perm[...], weigh_in[...].reshape(SLOTS, 128), preferred_element_type=F32).T.astype(BF)
    loads[6].wait()
    loads[7].wait()

    for d in (1, 2, 3):
        proj_copy(d).wait_recv()

    def att_copy(dy):
        return remote(att.at[0], att.at[dy], as_.at[dy - 1], ar.at[dy - 1], along_y(dy))

    for dy in (1, 2, 3):
        att_copy(dy).wait_recv()

    def core_part(j):
        return remote(part.at[j, 1 - core], other.at[j], d1s.at[j], d1r.at[j], partner)

    def x_copy(j, dx):
        i = j * 3 + dx - 1
        return remote(send_x.at[j, dx], from_x.at[j, dx - 1], d2s.at[i], d2r.at[i], along_x(dx))

    def yz_copy(j, dy, dz):
        i = j * 8 + dy * 2 + dz
        return remote(send_z.at[j, dy, dz], from_z.at[j, dy, dz], d3s.at[i], d3r.at[i], along_yz(dy, dz))

    def project(j):
        got = jnp.dot(att[...].reshape(1024, 512), proj[(z_lo + 4 - j) % 4], preferred_element_type=F32)
        got = got.astype(BF).reshape(4, 2, 4, 2, ROWS, 256)
        part[j, 0] = got[:, :, :, 0]
        part[j, 1] = got[:, :, :, 1]
        core_part(j).start()

    def sum_cores(j):
        core_part(j).wait_recv()
        for dx in (2, 1, 3, 0):
            xt = (x + dx) % 4
            for dz in range(2):
                zt = (z_hi + dz) % 2
                for dy in range(4):
                    mine = part[j, core, dy, zt, xt].astype(F32) + other[j, dy, zt, xt].astype(F32)
                    send_x[j, dx, dy, dz] = mine.astype(BF)
            if dx > 0:
                x_copy(j, dx).start()

    def sum_x(j):
        for dx in (1, 2, 3):
            x_copy(j, dx).wait_recv()
        for dz in (1, 0):
            for dy in (3, 2, 1, 0):
                got = send_x[j, 0, dy, dz].astype(F32) + from_x[j, 0, dy, dz].astype(F32)
                got = got + (from_x[j, 1, dy, dz].astype(F32) + from_x[j, 2, dy, dz].astype(F32))
                if dy + dz > 0:
                    send_z[j, dy, dz] = got.astype(BF)
                    yz_copy(j, dy, dz).start()
                else:
                    from_z[j, 0, 0] = got.astype(BF)

    def token_copy(c, d):
        return remote(tok.at[c, 0], tok.at[c, d], ts.at[c], tr.at[c], along_z(d))

    def all_tokens(c):
        return remote(tok.at[c, pl.ds(1, 7)], tok.at[c, pl.ds(1, 7)], ts.at[c], tr.at[c], partner)

    def sum_all(j, square):
        for dy in range(4):
            for dz in range(2):
                if dy + dz > 0:
                    yz_copy(j, dy, dz).wait_recv()
            ysrc = (y + dy) % 4
            cols = tile(j * 4 + ysrc)
            got = from_z[j, dy, 0].astype(F32) + from_z[j, dy, 1].astype(F32)
            state = (resid[:, cols].astype(F32) + got).astype(BF)
            hidden[:, cols] = state
            state = state.astype(F32)
            square = square + state * state
            per = CW // 256
            tok[j * SUB + ysrc // per, 0, :, tile(ysrc % per)] = (state * gain[:, cols]).astype(BF)
        for c in range(j * SUB, j * SUB + SUB):

            def one(d, _):
                token_copy(c, d).start()
                return 0

            lax.fori_loop(1, 8, one, 0)
        return square

    def all_rows(c):
        return remote(packed.at[c], rows.at[c, pl.ds(1, 15)], xs.at[c], xr.at[c], partner)

    def pack(j):
        def one(s, _):
            c = j * SUB + s
            all_tokens(c).wait_recv()

            def columns(n, _):
                got = jnp.dot(choose[...], tok[c, :, :, tile(n)].reshape(128, 256), preferred_element_type=F32)
                got = got.astype(BF).reshape(16, SLOT, 256)
                rows[c, 0, :, tile(n)] = got[0]
                packed[c, :, :, tile(n)] = got[1:]
                return 0

            lax.fori_loop(0, CW // 256, columns, 0)

            def send(i, _):
                remote(packed.at[c, i - 1], rows.at[c, i], xs.at[c], xr.at[c], in_plane(i)).start()
                return 0

            lax.fori_loop(1, 16, send, 0)
            return 0

        lax.fori_loop(0, SUB, one, 0)

    def scale_copy(d):
        return remote(scale.at[0], scale.at[d], ss.at[0], sr.at[0], along_z(d))

    def all_scales():
        return remote(scale.at[pl.ds(1, 7)], scale.at[pl.ds(1, 7)], ss.at[0], sr.at[0], partner)

    def all_slot_scales():
        return remote(scale_out, scale_in.at[pl.ds(1, 15)], ss.at[1], sr.at[1], partner)

    square = jnp.zeros((ROWS, 256), F32)
    for t in range(8):
        if t < 4:
            project(t)
        if 0 <= t - 1 < 4:
            sum_cores(t - 1)
        if 0 <= t - 2 < 4:
            sum_x(t - 2)
        if 0 <= t - 3 < 4:
            square = sum_all(t - 3, square)
        if t == 3:
            lax.fori_loop(0, NC, start_far, 0)
            far_d.start()
        if t == 6:
            mean = jnp.sum(square, axis=1, keepdims=True) * (1.0 / D)
            factor = jnp.broadcast_to(lax.rsqrt(mean + EPS), (ROWS, 128))
            coarse = factor.astype(BF)
            fine = (factor - coarse.astype(F32)).astype(BF)
            lane = lax.broadcasted_iota(jnp.int32, (ROWS, 128), 1)
            scale[0] = jnp.where(lane < 64, coarse.astype(F32), fine.astype(F32)).astype(BF)
            for d in range(1, 8):
                scale_copy(d).start()
        if 0 <= t - 4 < 4:
            pack(t - 4)

    all_scales().wait_recv()
    got = jnp.dot(choose[...], scale[...].reshape(128, 128), preferred_element_type=F32)
    got = got.astype(BF).reshape(16, SLOT, 128)
    scale_in[0] = got[0]
    scale_out[...] = got[1:]

    def send_scale(i, _):
        remote(scale_out.at[i - 1], scale_in.at[i], ss.at[1], sr.at[1], in_plane(i)).start()
        return 0

    lax.fori_loop(1, 16, send_scale, 0)

    acc_g[...] = jnp.zeros_like(acc_g)
    acc_u[...] = jnp.zeros_like(acc_u)

    def upward(c, _):
        local_g(c).wait()
        local_u(c).wait()
        far_g(c).wait_recv()
        far_u(c).wait_recv()
        all_rows(c).wait_recv()

        def columns(n, _):
            got = rows[c].reshape(SLOTS, CW)
            acc_g[:, tile(n)] += jnp.dot(got, wg[chunk(c), tile(n)], preferred_element_type=F32)
            acc_u[:, tile(n)] += jnp.dot(got, wu[chunk(c), tile(n)], preferred_element_type=F32)
            return 0

        lax.fori_loop(0, 3, columns, 0)
        return 0

    lax.fori_loop(0, NC, upward, 0)
    all_slot_scales().wait_recv()
    both = scale_in[...].reshape(SLOTS, 128).astype(F32)
    factor = both[:, 0:1] + both[:, 64:65]

    def activate(n, _):
        act[:, tile(n)] = (jax.nn.silu(acc_g[:, tile(n)] * factor) * (acc_u[:, tile(n)] * factor)).astype(BF)
        return 0

    lax.fori_loop(0, 3, activate, 0)
    local_d.wait()
    far_d.wait_recv()

    def all_back(c):
        return remote(back.at[c], ret.at[c, pl.ds(1, 15)], rs.at[c], rr.at[c], partner)

    def all_sums(c):
        return remote(summed.at[c, pl.ds(1, 7)], sums_in.at[c, pl.ds(1, 7)], fs.at[c], fr.at[c], partner)

    def downward(c, _):
        def columns(n, _):
            got = jnp.dot(act[...], wd[:, tile(c * (CW // 256) + n)], preferred_element_type=F32)
            got = got.astype(BF).reshape(16, SLOT, 256)
            ret[c, 0, :, tile(n)] = got[0]
            back[c, :, :, tile(n)] = got[1:]
            return 0

        lax.fori_loop(0, CW // 256, columns, 0)

        def send(i, _):
            remote(back.at[c, i - 1], ret.at[c, i], rs.at[c], rr.at[c], plane_back(i)).start()
            return 0

        lax.fori_loop(1, 16, send, 0)
        return 0

    lax.fori_loop(0, NC, downward, 0)

    def combine(c, _):
        all_back(c).wait_recv()

        def columns(n, _):
            got = ret[c, :, :, tile(n)].reshape(SLOTS, 256)
            got = jnp.dot(spread[...], got, preferred_element_type=F32)
            summed[c, :, :, tile(n)] = got.astype(BF).reshape(8, ROWS, 256)
            return 0

        lax.fori_loop(0, CW // 256, columns, 0)

        def send(d, _):
            remote(summed.at[c, d], sums_in.at[c, d], fs.at[c], fr.at[c], along_z(8 - d)).start()
            return 0

        lax.fori_loop(1, 8, send, 0)
        return 0

    lax.fori_loop(0, NC, combine, 0)

    def finish(c, _):
        all_sums(c).wait_recv()
        got = summed[c, 0].astype(F32)
        for d in range(1, 8):
            got = got + sums_in[c, d].astype(F32)
        out_ref[:, chunk(c)] = (hidden[:, chunk(c)].astype(F32) + got).astype(BF)
        return 0

    lax.fori_loop(0, NC, finish, 0)

    for d in (1, 2, 3):
        z_copy(d).wait_send()
        proj_copy(d).wait_send()
        att_copy(d).wait_send()
    for d in range(4):
        for dy in (1, 2, 3):
            y_copy(d, dy).wait_send()
        for dy in range(4):
            if d + dy > 0:
                core_copy(d, dy).wait_send()
    for j in range(4):
        core_part(j).wait_send()
        for dx in (1, 2, 3):
            x_copy(j, dx).wait_send()
        for dy in range(4):
            for dz in range(2):
                if dy + dz > 0:
                    yz_copy(j, dy, dz).wait_send()
    for c in all_picks():
        c.wait_send()
    all_scales().wait_send()
    all_slot_scales().wait_send()

    def drain(c, _):
        far_g(c).wait_send()
        far_u(c).wait_send()
        all_tokens(c).wait_send()
        all_rows(c).wait_send()
        all_back(c).wait_send()
        all_sums(c).wait_send()
        return 0

    lax.fori_loop(0, NC, drain, 0)
    far_d.wait_send()


def slot_order():
    perm = np.zeros((SLOTS, SLOTS), np.float32)
    for p in range(16):
        for s in range(8):
            for r in range(CAP):
                perm[p * SLOT + s * CAP + r, s * 16 * CAP + r * 16 + p] = 1.0
    return perm


VMEM = pl.BlockSpec(memory_space=pltpu.VMEM)
SMEM = pl.BlockSpec(memory_space=pltpu.SMEM)
ANY = pl.BlockSpec(memory_space=pl.ANY)
SHAPE = jax.ShapeDtypeStruct
DMA = pltpu.SemaphoreType.DMA


def both_ways(*counts):
    return [DMA((n,)) for n in counts for _ in range(2)]


def layer(*operands):
    return pl.pallas_call(
        layer_kernel,
        out_shape=SHAPE((ROWS, D), BF),
        in_specs=[SMEM] + [ANY] * 11,
        out_specs=VMEM,
        scratch_shapes=[
            pltpu.VMEM((256, 512), BF),
            pltpu.VMEM((ROWS, D), BF),
            pltpu.VMEM((1, D), F32),
            pltpu.VMEM((2 * TOP, 128), F32),
            pltpu.VMEM((SLOTS, SLOTS), BF),
            pltpu.VMEM((2, 4, 4, 272, HEAD), BF),
            pltpu.VMEM((4, 256, 256), F32),
            pltpu.VMEM((256, HEAD), F32),
            pltpu.VMEM((4, 256, HEAD), F32),
            pltpu.VMEM((4, 256, HEAD), F32),
            pltpu.VMEM((4, 256, HEAD), F32),
            pltpu.VMEM((4, 256, 512), BF),
            pltpu.VMEM((4, 512, 256), BF),
            pltpu.VMEM((4, 2, 4, 2, 4, ROWS, 256), BF),
            pltpu.VMEM((4, 4, 2, 4, ROWS, 256), BF),
            pltpu.VMEM((4, 4, 4, 2, ROWS, 256), BF),
            pltpu.VMEM((4, 3, 4, 2, ROWS, 256), BF),
            pltpu.VMEM((4, 4, 2, ROWS, 256), BF),
            pltpu.VMEM((4, 4, 2, ROWS, 256), BF),
            pltpu.VMEM((ROWS, D), BF),
            pltpu.VMEM((D, 2 * FH), BF),
            pltpu.VMEM((D, 2 * FH), BF),
            pltpu.VMEM((2 * FH, D), BF),
            pltpu.VMEM((8, CAP, 16, 128), BF),
            pltpu.VMEM((8, CAP, 16, 128), BF),
            pltpu.VMEM((8, CAP, 16, 128), BF),
            pltpu.VMEM((8, CAP, 16, 128), BF),
            pltpu.VMEM((SLOTS, 128), BF),
            pltpu.VMEM((128, SLOTS), BF),
            pltpu.VMEM((NC, 8, ROWS, CW), BF),
            pltpu.VMEM((8, ROWS, 128), BF),
            pltpu.VMEM((NC, 15, SLOT, CW), BF),
            pltpu.VMEM((NC, 16, SLOT, CW), BF),
            pltpu.VMEM((15, SLOT, 128), BF),
            pltpu.VMEM((16, SLOT, 128), BF),
            pltpu.VMEM((SLOTS, 2 * FH), F32),
            pltpu.VMEM((SLOTS, 2 * FH), F32),
            pltpu.VMEM((SLOTS, 2 * FH), BF),
            pltpu.VMEM((NC, 15, SLOT, CW), BF),
            pltpu.VMEM((NC, 16, SLOT, CW), BF),
            pltpu.VMEM((NC, 8, ROWS, CW), BF),
            pltpu.VMEM((NC, 8, ROWS, CW), BF),
            DMA((8,)),
            *both_ways(3, 12, 16, 3, 3, 4, 12, 32),
            DMA((NC,)), DMA((NC,)), DMA((1,)),
            *both_ways(NC, NC, 1, 2, NC, 2, NC, NC, NC),
        ],
        compiler_params=pltpu.CompilerParams(
            collective_id=0, has_side_effects=True, vmem_limit_bytes=60 * 1024 * 1024
        ),
        name="layer",
    )(*operands)


def local(
    queries,
    key_states,
    value_head_states,
    block_order,
    out_proj,
    residual,
    norm_gain,
    w_gate,
    w_up,
    w_down,
    routes,
    gate_weights,
):
    routing = jnp.concatenate([routes.astype(F32), gate_weights], axis=1)
    routing = jnp.tile(routing.T, (1, 8))
    perm = jnp.asarray(slot_order(), BF)
    return layer(
        block_order, queries, key_states, value_head_states, out_proj, residual,
        norm_gain.reshape(1, D), routing, perm, w_gate, w_up, w_down,
    )


def solution(mesh):
    return jax.shard_map(
        local,
        mesh=mesh,
        in_specs=(
            P("ctx", "ep"),
            P("ctx", None),
            P("ctx", None),
            P("ctx"),
            P("ep", "ctx"),
            P(("ctx", "ep"), None),
            P(),
            P(None, ("ctx", "ep")),
            P(None, ("ctx", "ep")),
            P(("ctx", "ep"), None),
            P(("ctx", "ep"), None),
            P(("ctx", "ep"), None),
        ),
        out_specs=P(("ctx", "ep"), None),
        check_vma=False,
    )
```

```python
import math

import jax
import jax.numpy as jnp
import numpy as np
from jax import lax
from jax.experimental import pallas as pl
from jax.experimental.pallas import tpu as pltpu
from jax.sharding import PartitionSpec as P

MESH = pl.DeviceIdType.MESH
BF = jnp.bfloat16
F32 = jnp.float32

D = 4096
HEAD = 128
TOP = 8
NEG = -1e30
EPS = 1e-06
SCALE2 = math.log2(math.e) / math.sqrt(HEAD)

SUB = 2
NC = 4 * SUB
CW = D // NC
ROWS = 16
CAP = 3
SLOT = 8 * CAP
SLOTS = 16 * SLOT
FH = 384


def here():
    c = lax.axis_index("ctx")
    e = lax.axis_index("ep")
    return (e // 2) % 4, c % 4, e // 8, c // 4, e % 2


def device(x, y, z_hi, z_lo, core):
    return (z_lo * 4 + y, z_hi * 8 + x * 2 + core)


def remote(src, dst, send, recv, target):
    return pltpu.make_async_remote_copy(
        src_ref=src, dst_ref=dst, send_sem=send, recv_sem=recv, device_id=target, device_id_type=MESH
    )


def layer_kernel(
    order_ref, q_hbm, k_hbm, v_hbm, proj_hbm, resid_hbm, gain_hbm, routes_hbm, gates_hbm, perm_hbm, wg_hbm, wu_hbm, wd_hbm,
    out_ref,
    query, resid, gain, routes, gates, perm,
    kv, scores, qpos, peak, total, acc, att, proj, part, other, send_x, from_x, send_z, from_z, hidden,
    wg, wu, wd, weigh, weigh_in, choose, spread,
    tok, scale, packed, rows, scale_out, scale_in, acc_g, acc_u, act, back, ret, summed, sums_in,
    load_sem, zs, zr, ys, yr, cs, cr, rights, rightr, lefts, leftr, as_, ar, d1s, d1r, d2s, d2r, d3s, d3r,
    lg, lu, ld, gs, gr, us, ur, ws, wr, os_, or_, ts, tr, ss, sr, xs, xr, rs, rr, fs, fr,
):
    x, y, z_hi, z_lo, core = here()
    z = z_hi * 4 + z_lo
    partner = device(x, y, z_hi, z_lo, 1 - core)

    def in_span(d):
        return device(x, y, z_hi, (z_lo + d) % 4, core)

    def along_y(d):
        return device(x, (y + d) % 4, z_hi, z_lo, core)

    def along_x(d):
        return device((x + d) % 4, y, z_hi, z_lo, core)

    def along_yz(dy, dz):
        return device(x, (y + 4 - dy) % 4, (z_hi + dz) % 2, z_lo, core)

    def along_z(d):
        to = (z + d) % 8
        return device(x, y, to // 4, to % 4, core)

    def in_plane(i):
        return device((x + i % 4) % 4, (y + i // 4) % 4, z_hi, z_lo, core)

    def plane_back(i):
        return device((x + 4 - i % 4) % 4, (y + 4 - i // 4) % 4, z_hi, z_lo, core)

    def chunk(c):
        return pl.ds(pl.multiple_of(c * CW, CW), CW)

    def tile(n):
        return pl.ds(pl.multiple_of(n * 256, 256), 256)

    head_col = pl.multiple_of((z_hi * 2 + x // 2) * HEAD, HEAD)
    loads = [
        pltpu.make_async_copy(src, dst, load_sem.at[i])
        for i, (src, dst) in enumerate([
            (k_hbm.at[:, pl.ds(head_col, HEAD)], kv.at[0, 0, 0, pl.ds(0, 256), :]),
            (v_hbm.at[:, pl.ds(head_col, HEAD)], kv.at[1, 0, 0, pl.ds(0, 256), :]),
            (proj_hbm, proj.at[z_lo]),
            (q_hbm, query),
            (routes_hbm, routes),
            (perm_hbm, perm),
            (resid_hbm, resid),
            (gain_hbm, gain),
            (gates_hbm, gates),
        ])
    ]
    for c in loads:
        c.start()

    barrier = pltpu.get_barrier_semaphore()

    def greet(target):
        pl.semaphore_signal(barrier, inc=1, device_id=target, device_id_type=MESH)

    def greet_z(d, _):
        greet(along_z(d))
        return 0

    def greet_plane(i, _):
        greet(in_plane(i))
        return 0

    greet(partner)
    lax.fori_loop(1, 8, greet_z, 0)
    lax.fori_loop(1, 16, greet_plane, 0)
    for dy in (1, 2, 3):
        greet(along_yz(dy, 1))

    first = order_ref[0].astype(F32)
    second = order_ref[1].astype(F32)
    row16 = lax.broadcasted_iota(jnp.int32, (16, HEAD), 0)
    tail = jnp.where(row16 < 8, first, second).astype(BF)
    kv[0, 0, 0, 256:272, :] = tail
    kv[1, 0, 0, 256:272, :] = tail
    row = lax.broadcasted_iota(jnp.int32, (256, HEAD), 0)
    qpos[...] = jnp.where(row < 128, first * 128.0 + row.astype(F32), (second - 1.0) * 128.0 + row.astype(F32))

    loads[0].wait()
    loads[1].wait()
    pl.semaphore_wait(barrier, 26)

    def z_copy(d):
        return remote(kv.at[core, 0, 0], kv.at[core, d, 0], zs.at[d - 1], zr.at[d - 1], in_span(d))

    def y_copy(d, dy):
        i = d * 3 + dy - 1
        return remote(kv.at[core, d, 0], kv.at[core, d, dy], ys.at[i], yr.at[i], along_y(dy))

    def core_copy(d, dy):
        i = d * 4 + dy
        return remote(kv.at[core, d, dy], kv.at[core, d, dy], cs.at[i], cr.at[i], partner)

    def core_arrival(d, dy):
        i = d * 4 + dy
        return remote(kv.at[1 - core, d, dy], kv.at[1 - core, d, dy], cs.at[i], cr.at[i], partner)

    def right_copy(p, slot):
        return remote(proj.at[slot], proj.at[slot], rights.at[p], rightr.at[p], in_span(1))

    def left_copy(p, slot):
        return remote(proj.at[slot], proj.at[slot], lefts.at[p], leftr.at[p], in_span(3))

    def proj_send(p):
        @pl.when((z_lo <= 2) & (z_lo >= p))
        def _():
            right_copy(p, z_lo - p).start()

        @pl.when((z_lo >= 1) & (z_lo + p <= 3))
        def _():
            left_copy(p, z_lo + p).start()

    def proj_arrival(p):
        @pl.when(z_lo >= p + 1)
        def _():
            right_copy(p, z_lo - 1 - p).wait_recv()

        @pl.when(z_lo <= 2 - p)
        def _():
            left_copy(p, z_lo + 1 + p).wait_recv()

    def proj_sent(p):
        @pl.when((z_lo <= 2) & (z_lo >= p))
        def _():
            right_copy(p, z_lo - p).wait_send()

        @pl.when((z_lo >= 1) & (z_lo + p <= 3))
        def _():
            left_copy(p, z_lo + p).wait_send()

    for d in (1, 2, 3):
        z_copy(d).start()
    for dy in (1, 2, 3):
        y_copy(0, dy).start()

    loads[4].wait()
    loads[8].wait()
    token = lax.broadcasted_iota(jnp.int32, (ROWS, 128), 0)
    lane = lax.broadcasted_iota(jnp.int32, (ROWS, 128), 1)
    repeat = jnp.where((lane & 15) == token, 1.0, 0.0)
    named_by = jnp.dot(routes[...].astype(F32), repeat, preferred_element_type=F32)
    weight_by = jnp.dot(gates[...], repeat, preferred_element_type=F32)
    row = lax.broadcasted_iota(jnp.int32, (128, 128), 0)
    lane = lax.broadcasted_iota(jnp.int32, (128, 128), 1)
    z_to = (z + (row >> 4)) & 7
    x_to = (x + (row & 3)) & 3
    y_to = (y + ((row >> 2) & 3)) & 3
    expert = ((z_to & 3) * 32 + y_to * 8 + (z_to >> 2) * 4 + x_to).astype(F32)
    own = (lane >> 4) == (row >> 4)
    named = jnp.zeros((128, 128), F32)
    weight = jnp.zeros((128, 128), F32)
    for j in range(TOP):
        hit = jnp.where(own & (jnp.abs(named_by[j : j + 1, :] - expert) < 0.5), 1.0, 0.0)
        named = named + hit
        weight = weight + hit * weight_by[j : j + 1, :]
    before = jnp.where(row < lane, 1.0, 0.0).astype(BF)
    rank = jnp.dot(named.astype(BF), before, preferred_element_type=F32)
    for r in range(CAP):
        at = jnp.where((named > 0.5) & (jnp.abs(rank - r) < 0.5), 1.0, 0.0)
        weigh[:, r] = (at * weight).reshape(8, 16, 128).astype(BF)

    for d in (1, 2, 3):
        z_copy(d).wait_recv()
        if d == 1:
            loads[2].wait()
            proj_send(0)
        for dy in (1, 2, 3):
            y_copy(d, dy).start()
        core_copy(d, 0).start()
    def weigh_copy(d):
        return remote(weigh.at[d], weigh_in.at[d], os_.at[0], or_.at[0], along_z(d))

    def all_weigh():
        return remote(weigh.at[pl.ds(1, 7)], weigh_in.at[pl.ds(1, 7)], os_.at[0], or_.at[0], partner)

    def send_weigh(d, _):
        weigh_copy(d).start()
        return 0

    weigh_in[0] = weigh[0]

    own_half = pl.ds(0, FH)
    far_half = pl.ds(FH, FH)

    def from_rows(f, b):
        return pl.ds(pl.multiple_of((b * 4 + f) * 256, 256), 256)

    def local_weights(f):
        for b in range(4):
            pltpu.make_async_copy(wg_hbm.at[from_rows(f, b), :], wg.at[f, pl.ds(b * 256, 256), own_half], lg.at[f]).start()
            pltpu.make_async_copy(wu_hbm.at[from_rows(f, b), :], wu.at[f, pl.ds(b * 256, 256), own_half], lu.at[f]).start()

    def far_weights(f):
        for b in range(4):
            remote(wg_hbm.at[from_rows(f, b), :], wg.at[f, pl.ds(b * 256, 256), far_half], gs.at[f], gr.at[f], partner).start()
            remote(wu_hbm.at[from_rows(f, b), :], wu.at[f, pl.ds(b * 256, 256), far_half], us.at[f], ur.at[f], partner).start()

    def all_local(f):
        return (
            pltpu.make_async_copy(wg_hbm.at[pl.ds(0, 1024), :], wg.at[f, :, own_half], lg.at[f]),
            pltpu.make_async_copy(wu_hbm.at[pl.ds(0, 1024), :], wu.at[f, :, own_half], lu.at[f]),
        )

    def all_far(f):
        return (
            remote(wg_hbm.at[pl.ds(0, 1024), :], wg.at[f, :, far_half], gs.at[f], gr.at[f], partner),
            remote(wu_hbm.at[pl.ds(0, 1024), :], wu.at[f, :, far_half], us.at[f], ur.at[f], partner),
        )

    local_d = pltpu.make_async_copy(wd_hbm, wd.at[own_half, :], ld.at[0])
    far_d = remote(wd_hbm, wd.at[far_half, :], ws.at[0], wr.at[0], partner)

    def start_local(f, _):
        local_weights(f)
        return 0

    def start_far(f, _):
        far_weights(f)
        return 0

    lanes = lax.broadcasted_iota(jnp.int32, (8, HEAD), 1).astype(F32)
    loads[3].wait()

    def group(d, last):
        for dy in range(4):
            if d + dy > 0:
                core_arrival(d, dy).wait_recv()

        def score(h, side):
            q = query[:, pl.ds(pl.multiple_of(h * HEAD, HEAD), HEAD)]
            top = None
            for dy in range(4):
                ids = kv[0, d, dy, 256:272, :].astype(F32) * 128.0
                got = lax.dot_general(
                    q, kv[0, d, dy, 0:256, :], (((1,), (1,)), ((), ())), preferred_element_type=F32
                )
                left = jnp.where((ids[0:8] + lanes)[0:1] <= qpos[...], got[:, :HEAD], NEG)
                right = jnp.where((ids[8:16] + lanes)[0:1] <= qpos[...], got[:, HEAD:], NEG)
                scores[side, dy, :, 0:HEAD] = left
                scores[side, dy, :, HEAD:256] = right
                both = jnp.maximum(left, right)
                top = both if top is None else jnp.maximum(top, both)
            return jnp.broadcast_to(jnp.max(top, axis=1, keepdims=True), (256, HEAD))

        def gather(h, side, now):
            cols = pl.ds(pl.multiple_of(h * HEAD, HEAD), HEAD)
            if d > 0:
                old = peak[h]
                now = jnp.maximum(now, old)
                shrink = jnp.exp2((old - now) * SCALE2)
                sums = total[h] * shrink
                out = acc[h] * shrink
            else:
                sums = jnp.zeros((256, HEAD), F32)
                out = jnp.zeros((256, HEAD), F32)
            peak[h] = now
            for dy in range(4):
                left = jnp.exp2((scores[side, dy, :, 0:HEAD] - now) * SCALE2)
                right = jnp.exp2((scores[side, dy, :, HEAD:256] - now) * SCALE2)
                both = jnp.concatenate([left.astype(BF), right.astype(BF)], axis=1)
                out = out + jnp.dot(both, kv[1, d, dy, 0:256, :], preferred_element_type=F32)
                sums = sums + (left + right)
            if last:
                att[0, :, cols] = (out / jnp.sum(sums, axis=1, keepdims=True)).astype(BF)
                for dy in (1, 3, 2):
                    remote(att.at[0, :, cols], att.at[dy, :, cols], as_.at[dy - 1], ar.at[dy - 1], along_y(dy)).start()
            else:
                total[h] = sums
                acc[h] = out

        def two_heads(i, _):
            even = score(2 * i, 0)
            odd = score(2 * i + 1, 1)
            gather(2 * i, 0, even)
            gather(2 * i + 1, 1, odd)
            return 0

        lax.fori_loop(0, 2, two_heads, 0)

    for d in range(4):
        for dy in (1, 2, 3):
            y_copy(d, dy).wait_recv()
            core_copy(d, dy).start()
        if d == 0:
            lax.fori_loop(0, 4, start_local, 0)
            local_d.start()
        else:
            if d == 1 or d == 3:
                proj_arrival(d // 2)
                proj_send(d // 2 + 1)
            group(d - 1, False)
    group(3, True)
    lax.fori_loop(1, 8, send_weigh, 0)

    def att_copy(dy):
        return remote(att.at[0], att.at[dy], as_.at[dy - 1], ar.at[dy - 1], along_y(dy))

    def core_part(dy):
        return remote(part.at[dy, 1 - core], other.at[dy], d1s.at[dy], d1r.at[dy], partner)

    def x_copy(dy, dx):
        i = dy * 3 + dx - 1
        return remote(send_x.at[dy, dx], from_x.at[dy, dx - 1], d2s.at[i], d2r.at[i], along_x(dx))

    def yz_copy(dy, dz):
        i = dy * 2 + dz
        return remote(send_z.at[dy, dz], from_z.at[dy, dz], d3s.at[i], d3r.at[i], along_yz(dy, dz))

    def project(dy):
        if dy > 0:
            att_copy(dy).wait_recv()
        for b in range(4):
            got = jnp.dot(att[dy], proj[b], preferred_element_type=F32)
            got = got.astype(BF).reshape(2, 4, 2, ROWS, 256)
            part[dy, 0, :, :, :, b * 256 : b * 256 + 256] = got[:, :, 0]
            part[dy, 1, :, :, :, b * 256 : b * 256 + 256] = got[:, :, 1]
        core_part(dy).start()

    def sum_cores(dy):
        core_part(dy).wait_recv()
        for dx in (2, 1, 3, 0):
            xt = (x + dx) % 4
            for dz in range(2):
                zt = (z_hi + dz) % 2
                mine = part[dy, core, zt, xt].astype(F32) + other[dy, zt, xt].astype(F32)
                send_x[dy, dx, dz] = mine.astype(BF)
            if dx > 0:
                x_copy(dy, dx).start()

    def sum_x(dy):
        for dx in (1, 2, 3):
            x_copy(dy, dx).wait_recv()
        for dz in (1, 0):
            got = send_x[dy, 0, dz].astype(F32) + from_x[dy, 0, dz].astype(F32)
            got = got + (from_x[dy, 1, dz].astype(F32) + from_x[dy, 2, dz].astype(F32))
            if dy + dz > 0:
                send_z[dy, dz] = got.astype(BF)
                yz_copy(dy, dz).start()
            else:
                from_z[0, 0] = got.astype(BF)

    def token_copy(dy, slot, step):
        to = (slot + step) % 8
        return remote(
            tok.at[dy, slot], tok.at[dy, to], ts.at[dy * 8 + to], tr.at[dy * 8 + to], along_z(1 if step == 1 else 7)
        )

    def last_step(dy):
        return (3, 1) if dy % 2 == 0 else (5, 7)

    def token_moves(dy):
        return [[(0, 1), (0, 7)], [(1, 1), (7, 7)], [(2, 1), (6, 7)], [last_step(dy)]]

    def forward(dy, hop):
        for slot, step in token_moves(dy)[hop - 1]:
            if hop > 1:
                token_copy(dy, (slot - step) % 8, step).wait_recv()
            token_copy(dy, slot, step).start()

    def sum_all(dy, square):
        for dz in range(2):
            if dy + dz > 0:
                yz_copy(dy, dz).wait_recv()
        from_y = (y + dy) % 4
        for b in range(4):
            cols = tile(b * 4 + from_y)
            near = slice(b * 256, b * 256 + 256)
            got = from_z[dy, 0, :, near].astype(F32) + from_z[dy, 1, :, near].astype(F32)
            state = (resid[:, cols].astype(F32) + got).astype(BF)
            hidden[:, cols] = state
            state = state.astype(F32)
            square = square + state * state
            tok[dy, 0, :, near] = (state * gain[:, cols]).astype(BF)
        forward(dy, 1)
        return square

    def all_rows(c):
        return remote(packed.at[c], rows.at[c, pl.ds(1, 15)], xs.at[c], xr.at[c], partner)

    def pack(dy):
        slot, step = last_step(dy)
        token_copy(dy, slot, step).wait_recv()
        slot, step = token_moves(dy)[2][1 if dy % 2 == 0 else 0]
        token_copy(dy, slot, step).wait_recv()

        def one(s, _):
            c = dy * SUB + s

            def columns(n, _):
                got = tok[dy, :, :, tile(s * (CW // 256) + n)].reshape(128, 256)
                got = jnp.dot(choose[...], got, preferred_element_type=F32)
                got = got.astype(BF).reshape(16, SLOT, 256)
                rows[c, 0, :, tile(n)] = got[0]
                packed[c, :, :, tile(n)] = got[1:]
                return 0

            lax.fori_loop(0, CW // 256, columns, 0)

            def send(i, _):
                remote(packed.at[c, i - 1], rows.at[c, i], xs.at[c], xr.at[c], in_plane(i)).start()
                return 0

            lax.fori_loop(1, 16, send, 0)
            return 0

        lax.fori_loop(0, SUB, one, 0)

    def scale_copy(d):
        return remote(scale.at[0], scale.at[d], ss.at[0], sr.at[0], along_z(d))

    def all_scales():
        return remote(scale.at[pl.ds(1, 7)], scale.at[pl.ds(1, 7)], ss.at[0], sr.at[0], partner)

    def all_slot_scales():
        return remote(scale_out, scale_in.at[pl.ds(1, 15)], ss.at[1], sr.at[1], partner)

    loads[5].wait()
    loads[6].wait()
    loads[7].wait()
    proj_arrival(2)
    square = jnp.zeros((ROWS, 256), F32)
    project(0)

    all_weigh().wait_recv()
    slots = jnp.dot(perm[...], weigh_in[...].reshape(SLOTS, 128), preferred_element_type=F32)
    choose[...] = jnp.where(slots > 0.0, 1.0, 0.0).astype(BF)
    spread[...] = slots.T.astype(BF)

    sum_cores(0)
    project(1)
    sum_x(0)
    sum_cores(1)
    project(3)
    sum_x(1)
    sum_cores(3)
    square = sum_all(0, square)
    project(2)
    forward(0, 2)
    sum_x(3)
    sum_cores(2)
    square = sum_all(1, square)
    forward(0, 3)
    forward(1, 2)
    forward(0, 4)
    sum_x(2)
    square = sum_all(3, square)
    forward(1, 3)
    forward(3, 2)
    pack(0)
    lax.fori_loop(0, 4, start_far, 0)
    far_d.start()
    forward(1, 4)
    square = sum_all(2, square)
    forward(3, 3)
    forward(2, 2)
    pack(1)
    forward(3, 4)
    forward(2, 3)
    mean = jnp.sum(square, axis=1, keepdims=True) * (1.0 / D)
    factor = jnp.broadcast_to(lax.rsqrt(mean + EPS), (ROWS, 128))
    coarse = factor.astype(BF)
    fine = (factor - coarse.astype(F32)).astype(BF)
    lane = lax.broadcasted_iota(jnp.int32, (ROWS, 128), 1)
    scale[0] = jnp.where(lane < 64, coarse.astype(F32), fine.astype(F32)).astype(BF)
    for d in range(1, 8):
        scale_copy(d).start()
    pack(3)
    forward(2, 4)
    pack(2)

    all_scales().wait_recv()
    got = jnp.dot(choose[...], scale[...].reshape(128, 128), preferred_element_type=F32)
    got = got.astype(BF).reshape(16, SLOT, 128)
    scale_in[0] = got[0]
    scale_out[...] = got[1:]

    def send_scale(i, _):
        remote(scale_out.at[i - 1], scale_in.at[i], ss.at[1], sr.at[1], in_plane(i)).start()
        return 0

    lax.fori_loop(1, 16, send_scale, 0)

    acc_g[...] = jnp.zeros_like(acc_g)
    acc_u[...] = jnp.zeros_like(acc_u)

    def weights_here(f, _):
        for c in all_local(f):
            c.wait()
        for c in all_far(f):
            c.wait_recv()
        return 0

    lax.fori_loop(0, 4, weights_here, 0)

    def upward(s, dy):
        c = dy * SUB + s
        all_rows(c).wait_recv()

        def one(q, _):
            f = (y + 4 - q + dy) % 4
            got = rows[c, pl.ds(q * 4, 4)].reshape(4 * SLOT, CW)
            at = pl.ds(pl.multiple_of(q * 4 * SLOT, 4 * SLOT), 4 * SLOT)
            depth = pl.ds(pl.multiple_of(s * CW, CW), CW)
            for n in range(3):
                cols = slice(n * 256, n * 256 + 256)
                acc_g[at, cols] += jnp.dot(got, wg[f, depth, cols], preferred_element_type=F32)
                acc_u[at, cols] += jnp.dot(got, wu[f, depth, cols], preferred_element_type=F32)
            return 0

        lax.fori_loop(0, 4, one, 0)
        return dy

    for dy in (0, 1, 3, 2):
        lax.fori_loop(0, SUB, upward, dy)
    all_slot_scales().wait_recv()
    both = scale_in[...].reshape(SLOTS, 128).astype(F32)
    factor = both[:, 0:1] + both[:, 64:65]

    def activate(n, _):
        act[:, tile(n)] = (jax.nn.silu(acc_g[:, tile(n)] * factor) * (acc_u[:, tile(n)] * factor)).astype(BF)
        return 0

    lax.fori_loop(0, 3, activate, 0)
    local_d.wait()
    far_d.wait_recv()

    def all_back(c):
        return remote(back.at[c], ret.at[c, pl.ds(1, 15)], rs.at[c], rr.at[c], partner)

    def all_sums(c):
        return remote(summed.at[c, pl.ds(1, 7)], sums_in.at[c, pl.ds(1, 7)], fs.at[c], fr.at[c], partner)

    def downward(c, _):
        def columns(n, _):
            got = jnp.dot(act[...], wd[:, tile(c * (CW // 256) + n)], preferred_element_type=F32)
            got = got.astype(BF).reshape(16, SLOT, 256)
            ret[c, 0, :, tile(n)] = got[0]
            back[c, :, :, tile(n)] = got[1:]
            return 0

        lax.fori_loop(0, CW // 256, columns, 0)

        def send(i, _):
            remote(back.at[c, i - 1], ret.at[c, i], rs.at[c], rr.at[c], plane_back(i)).start()
            return 0

        lax.fori_loop(1, 16, send, 0)
        return 0

    lax.fori_loop(0, NC, downward, 0)

    def combine(c, _):
        all_back(c).wait_recv()

        def columns(n, _):
            got = ret[c, :, :, tile(n)].reshape(SLOTS, 256)
            got = jnp.dot(spread[...], got, preferred_element_type=F32)
            summed[c, :, :, tile(n)] = got.astype(BF).reshape(8, ROWS, 256)
            return 0

        lax.fori_loop(0, CW // 256, columns, 0)

        def send(d, _):
            remote(summed.at[c, d], sums_in.at[c, d], fs.at[c], fr.at[c], along_z(8 - d)).start()
            return 0

        lax.fori_loop(1, 8, send, 0)
        return 0

    lax.fori_loop(0, NC, combine, 0)

    def finish(c, _):
        all_sums(c).wait_recv()
        got = summed[c, 0].astype(F32)
        for d in range(1, 8):
            got = got + sums_in[c, d].astype(F32)
        out_ref[:, chunk(c)] = (hidden[:, chunk(c)].astype(F32) + got).astype(BF)
        return 0

    lax.fori_loop(0, NC, finish, 0)

    for d in (1, 2, 3):
        z_copy(d).wait_send()
        proj_sent(d - 1)
        att_copy(d).wait_send()
    for d in range(4):
        for dy in (1, 2, 3):
            y_copy(d, dy).wait_send()
        for dy in range(4):
            if d + dy > 0:
                core_copy(d, dy).wait_send()
    for dy in range(4):
        core_part(dy).wait_send()
        for dx in (1, 2, 3):
            x_copy(dy, dx).wait_send()
        for dz in range(2):
            if dy + dz > 0:
                yz_copy(dy, dz).wait_send()
        for moves in token_moves(dy):
            for slot, step in moves:
                token_copy(dy, slot, step).wait_send()
        for c in all_far(dy):
            c.wait_send()
    all_weigh().wait_send()
    all_scales().wait_send()
    all_slot_scales().wait_send()

    def drain(c, _):
        all_rows(c).wait_send()
        all_back(c).wait_send()
        all_sums(c).wait_send()
        return 0

    lax.fori_loop(0, NC, drain, 0)
    far_d.wait_send()


def slot_order():
    perm = np.zeros((SLOTS, SLOTS), np.float32)
    for p in range(16):
        for s in range(8):
            for r in range(CAP):
                perm[p * SLOT + s * CAP + r, s * 16 * CAP + r * 16 + p] = 1.0
    return perm


VMEM = pl.BlockSpec(memory_space=pltpu.VMEM)
SMEM = pl.BlockSpec(memory_space=pltpu.SMEM)
ANY = pl.BlockSpec(memory_space=pl.ANY)
SHAPE = jax.ShapeDtypeStruct
DMA = pltpu.SemaphoreType.DMA


def both_ways(*counts):
    return [DMA((n,)) for n in counts for _ in range(2)]


def layer(*operands):
    return pl.pallas_call(
        layer_kernel,
        out_shape=SHAPE((ROWS, D), BF),
        in_specs=[SMEM] + [ANY] * 12,
        out_specs=VMEM,
        scratch_shapes=[
            pltpu.VMEM((256, 512), BF),
            pltpu.VMEM((ROWS, D), BF),
            pltpu.VMEM((1, D), F32),
            pltpu.VMEM((TOP, ROWS), jnp.int32),
            pltpu.VMEM((TOP, ROWS), F32),
            pltpu.VMEM((SLOTS, SLOTS), BF),
            pltpu.VMEM((2, 4, 4, 272, HEAD), BF),
            pltpu.VMEM((2, 4, 256, 256), F32),
            pltpu.VMEM((256, HEAD), F32),
            pltpu.VMEM((4, 256, HEAD), F32),
            pltpu.VMEM((4, 256, HEAD), F32),
            pltpu.VMEM((4, 256, HEAD), F32),
            pltpu.VMEM((4, 256, 512), BF),
            pltpu.VMEM((4, 512, 256), BF),
            pltpu.VMEM((4, 2, 2, 4, ROWS, 1024), BF),
            pltpu.VMEM((4, 2, 4, ROWS, 1024), BF),
            pltpu.VMEM((4, 4, 2, ROWS, 1024), BF),
            pltpu.VMEM((4, 3, 2, ROWS, 1024), BF),
            pltpu.VMEM((4, 2, ROWS, 1024), BF),
            pltpu.VMEM((4, 2, ROWS, 1024), BF),
            pltpu.VMEM((ROWS, D), BF),
            pltpu.VMEM((4, 1024, 2 * FH), BF),
            pltpu.VMEM((4, 1024, 2 * FH), BF),
            pltpu.VMEM((2 * FH, D), BF),
            pltpu.VMEM((8, CAP, 16, 128), BF),
            pltpu.VMEM((8, CAP, 16, 128), BF),
            pltpu.VMEM((SLOTS, 128), BF),
            pltpu.VMEM((128, SLOTS), BF),
            pltpu.VMEM((4, 8, ROWS, 1024), BF),
            pltpu.VMEM((8, ROWS, 128), BF),
            pltpu.VMEM((NC, 15, SLOT, CW), BF),
            pltpu.VMEM((NC, 16, SLOT, CW), BF),
            pltpu.VMEM((15, SLOT, 128), BF),
            pltpu.VMEM((16, SLOT, 128), BF),
            pltpu.VMEM((SLOTS, 2 * FH), F32),
            pltpu.VMEM((SLOTS, 2 * FH), F32),
            pltpu.VMEM((SLOTS, 2 * FH), BF),
            pltpu.VMEM((NC, 15, SLOT, CW), BF),
            pltpu.VMEM((NC, 16, SLOT, CW), BF),
            pltpu.VMEM((NC, 8, ROWS, CW), BF),
            pltpu.VMEM((NC, 8, ROWS, CW), BF),
            DMA((9,)),
            *both_ways(3, 12, 16, 3, 3, 3, 4, 12, 8),
            DMA((4,)), DMA((4,)), DMA((1,)),
            *both_ways(4, 4, 1, 1, 32, 2, NC, NC, NC),
        ],
        compiler_params=pltpu.CompilerParams(
            collective_id=0, has_side_effects=True, vmem_limit_bytes=60 * 1024 * 1024
        ),
        name="layer",
    )(*operands)


def local(
    queries,
    key_states,
    value_head_states,
    block_order,
    out_proj,
    residual,
    norm_gain,
    w_gate,
    w_up,
    w_down,
    routes,
    gate_weights,
):
    perm = jnp.asarray(slot_order(), BF)
    return layer(
        block_order, queries, key_states, value_head_states, out_proj, residual,
        norm_gain.reshape(1, D), routes.T, gate_weights.T, perm, w_gate, w_up, w_down,
    )


def solution(mesh):
    return jax.shard_map(
        local,
        mesh=mesh,
        in_specs=(
            P("ctx", "ep"),
            P("ctx", None),
            P("ctx", None),
            P("ctx"),
            P("ep", "ctx"),
            P(("ctx", "ep"), None),
            P(),
            P(None, ("ctx", "ep")),
            P(None, ("ctx", "ep")),
            P(("ctx", "ep"), None),
            P(("ctx", "ep"), None),
            P(("ctx", "ep"), None),
        ),
        out_specs=P(("ctx", "ep"), None),
        check_vma=False,
    )
```

```python
import math

import jax
import jax.numpy as jnp
import numpy as np
from jax import lax
from jax.experimental import pallas as pl
from jax.experimental.pallas import tpu as pltpu
from jax.sharding import PartitionSpec as P

MESH = pl.DeviceIdType.MESH
BF = jnp.bfloat16
F32 = jnp.float32

D = 4096
HEAD = 128
TOP = 8
NEG = -1e30
EPS = 1e-06
SCALE2 = math.log2(math.e) / math.sqrt(HEAD)

SUB = 2
NC = 4 * SUB
CW = D // NC
ROWS = 16
CAP = 3
SLOT = 8 * CAP
SLOTS = 16 * SLOT
FH = 384
FAR_FIRST = sorted(range(1, 16), key=lambda i: -(min(i // 4, 4 - i // 4) + min(i % 4, 4 - i % 4)))


def here():
    c = lax.axis_index("ctx")
    e = lax.axis_index("ep")
    return (e // 2) % 4, c % 4, e // 8, c // 4, e % 2


def device(x, y, z_hi, z_lo, core):
    return (z_lo * 4 + y, z_hi * 8 + x * 2 + core)


def remote(src, dst, send, recv, target):
    return pltpu.make_async_remote_copy(
        src_ref=src, dst_ref=dst, send_sem=send, recv_sem=recv, device_id=target, device_id_type=MESH
    )


def layer_kernel(
    order_ref, q_hbm, k_hbm, v_hbm, proj_hbm, resid_hbm, gain_hbm, routes_hbm, gates_hbm, perm_hbm, wg_hbm, wu_hbm, wd_hbm,
    out_ref,
    query, resid, gain, routes, gates, perm,
    kv, scores, qpos, peak, total, acc, att, proj, part, other, send_x, from_x, send_z, from_z, hidden,
    wg, wu, wd, weigh, weigh_in, choose, spread,
    tok, scale, packed, rows, scale_out, scale_in, acc_g, acc_u, act, back, ret, summed, sums_in,
    load_sem, zs, zr, ys, yr, cs, cr, rights, rightr, lefts, leftr, as_, ar, d1s, d1r, d2s, d2r, d3s, d3r,
    lg, lu, ld, gs, gr, us, ur, ws, wr, os_, or_, ts, tr, ss, sr, xs, xr, rs, rr, fs, fr,
):
    x, y, z_hi, z_lo, core = here()
    z = z_hi * 4 + z_lo
    partner = device(x, y, z_hi, z_lo, 1 - core)

    def ahead(at, d, size):
        return lax.rem(at + d, size) if d else at

    ctx_at = [z_lo * 4 + ahead(y, d, 4) for d in range(4)]
    ep_at = [z_hi * 8 + ahead(x, d, 4) * 2 + core for d in range(4)]
    spans = [(ahead(z_lo, d, 4) * 4 + y, ep_at[0]) for d in range(4)]
    across = (1 - z_hi) * 8 + x * 2 + core
    columns_at = [
        (lax.rem(ahead(z, d, 8), 4) * 4 + y, (ahead(z, d, 8) // 4) * 8 + x * 2 + core) for d in range(8)
    ]

    def in_span(d):
        return spans[d]

    def along_y(d):
        return (ctx_at[d], ep_at[0])

    def along_x(d):
        return (ctx_at[0], ep_at[d])

    def along_yz(dy, dz):
        return (ctx_at[(4 - dy) % 4], across if dz else ep_at[0])

    def along_z(d):
        return columns_at[d % 8]

    def in_plane(i):
        return (ctx_at[i // 4], ep_at[i % 4])

    def plane_back(i):
        return (ctx_at[(4 - i // 4) % 4], ep_at[(4 - i % 4) % 4])

    def chunk(c):
        return pl.ds(pl.multiple_of(c * CW, CW), CW)

    def tile(n):
        return pl.ds(pl.multiple_of(n * 256, 256), 256)

    head_col = pl.multiple_of((z_hi * 2 + x // 2) * HEAD, HEAD)
    loads = [
        pltpu.make_async_copy(src, dst, load_sem.at[i])
        for i, (src, dst) in enumerate([
            (k_hbm.at[:, pl.ds(head_col, HEAD)], kv.at[0, 0, 0, pl.ds(0, 256), :]),
            (v_hbm.at[:, pl.ds(head_col, HEAD)], kv.at[1, 0, 0, pl.ds(0, 256), :]),
            (proj_hbm, proj.at[z_lo]),
            (q_hbm, query),
            (routes_hbm, routes),
            (perm_hbm, perm),
            (resid_hbm, resid),
            (gain_hbm, gain),
            (gates_hbm, gates),
        ])
    ]
    for c in loads:
        c.start()

    barrier = pltpu.get_barrier_semaphore()

    def greet(target):
        pl.semaphore_signal(barrier, inc=1, device_id=target, device_id_type=MESH)

    greet(partner)
    for d in range(1, 8):
        greet(along_z(d))
    for i in range(1, 16):
        greet(in_plane(i))
    for dy in (1, 2, 3):
        greet(along_yz(dy, 1))

    first = order_ref[0].astype(F32)
    second = order_ref[1].astype(F32)
    row16 = lax.broadcasted_iota(jnp.int32, (16, HEAD), 0)
    tail = jnp.where(row16 < 8, first, second).astype(BF)
    kv[0, 0, 0, 256:272, :] = tail
    kv[1, 0, 0, 256:272, :] = tail
    row = lax.broadcasted_iota(jnp.int32, (256, HEAD), 0)
    qpos[...] = jnp.where(row < 128, first * 128.0 + row.astype(F32), (second - 1.0) * 128.0 + row.astype(F32))

    loads[0].wait()
    loads[1].wait()
    own_half = pl.ds(0, FH)
    far_half = pl.ds(FH, FH)

    def local_weights(f):
        return (
            pltpu.make_async_copy(wg_hbm.at[:, f], wg.at[f, :, :, own_half], lg.at[f]),
            pltpu.make_async_copy(wu_hbm.at[:, f], wu.at[f, :, :, own_half], lu.at[f]),
        )

    def far_weights(f):
        return (
            remote(wg_hbm.at[:, f], wg.at[f, :, :, far_half], gs.at[f], gr.at[f], partner),
            remote(wu_hbm.at[:, f], wu.at[f, :, :, far_half], us.at[f], ur.at[f], partner),
        )

    local_d = pltpu.make_async_copy(wd_hbm, wd.at[own_half, :], ld.at[0])
    far_d = remote(wd_hbm, wd.at[far_half, :], ws.at[0], wr.at[0], partner)

    def start_far(f):
        for c in far_weights(f):
            c.start()

    for f in range(4):
        for c in local_weights(f):
            c.start()
    local_d.start()

    pl.semaphore_wait(barrier, 26)

    def z_copy(d):
        return remote(kv.at[core, 0, 0], kv.at[core, d, 0], zs.at[d - 1], zr.at[d - 1], in_span(d))

    def y_copy(d, dy):
        i = d * 3 + dy - 1
        return remote(kv.at[core, d, 0], kv.at[core, d, dy], ys.at[i], yr.at[i], along_y(dy))

    def core_copy(d, dy):
        i = d * 4 + dy
        return remote(kv.at[core, d, dy], kv.at[core, d, dy], cs.at[i], cr.at[i], partner)

    def core_arrival(d, dy):
        i = d * 4 + dy
        return remote(kv.at[1 - core, d, dy], kv.at[1 - core, d, dy], cs.at[i], cr.at[i], partner)

    def right_copy(p, slot):
        return remote(proj.at[slot], proj.at[slot], rights.at[p], rightr.at[p], in_span(1))

    def left_copy(p, slot):
        return remote(proj.at[slot], proj.at[slot], lefts.at[p], leftr.at[p], in_span(3))

    def proj_send(p):
        @pl.when((z_lo <= 2) & (z_lo >= p))
        def _():
            right_copy(p, z_lo - p).start()

        @pl.when((z_lo >= 1) & (z_lo + p <= 3))
        def _():
            left_copy(p, z_lo + p).start()

    def proj_arrival(p):
        @pl.when(z_lo >= p + 1)
        def _():
            right_copy(p, z_lo - 1 - p).wait_recv()

        @pl.when(z_lo <= 2 - p)
        def _():
            left_copy(p, z_lo + 1 + p).wait_recv()

    def proj_sent(p):
        @pl.when((z_lo <= 2) & (z_lo >= p))
        def _():
            right_copy(p, z_lo - p).wait_send()

        @pl.when((z_lo >= 1) & (z_lo + p <= 3))
        def _():
            left_copy(p, z_lo + p).wait_send()

    for d in (1, 2, 3):
        z_copy(d).start()
    for dy in (1, 2, 3):
        y_copy(0, dy).start()

    loads[4].wait()
    loads[8].wait()
    token = lax.broadcasted_iota(jnp.int32, (ROWS, 128), 0)
    lane = lax.broadcasted_iota(jnp.int32, (ROWS, 128), 1)
    repeat = jnp.where((lane & 15) == token, 1.0, 0.0)
    named_by = jnp.dot(routes[...].astype(F32), repeat, preferred_element_type=F32)
    weight_by = jnp.dot(gates[...], repeat, preferred_element_type=F32)
    row = lax.broadcasted_iota(jnp.int32, (128, 128), 0)
    lane = lax.broadcasted_iota(jnp.int32, (128, 128), 1)
    z_to = (z + (row >> 4)) & 7
    x_to = (x + (row & 3)) & 3
    y_to = (y + ((row >> 2) & 3)) & 3
    expert = ((z_to & 3) * 32 + y_to * 8 + (z_to >> 2) * 4 + x_to).astype(F32)
    own = (lane >> 4) == (row >> 4)
    named = jnp.zeros((128, 128), F32)
    weight = jnp.zeros((128, 128), F32)
    for j in range(TOP):
        hit = jnp.where(own & (jnp.abs(named_by[j : j + 1, :] - expert) < 0.5), 1.0, 0.0)
        named = named + hit
        weight = weight + hit * weight_by[j : j + 1, :]
    before = jnp.where(row < lane, 1.0, 0.0).astype(BF)
    rank = jnp.dot(named.astype(BF), before, preferred_element_type=F32)
    for r in range(CAP):
        at = jnp.where((named > 0.5) & (jnp.abs(rank - r) < 0.5), 1.0, 0.0)
        weigh[:, r] = (at * weight).reshape(8, 16, 128).astype(BF)

    for d in (1, 2, 3):
        z_copy(d).wait_recv()
        if d == 1:
            loads[2].wait()
            proj_send(0)
        for dy in (1, 2, 3):
            y_copy(d, dy).start()
        core_copy(d, 0).start()
    def weigh_copy(d):
        return remote(weigh.at[d], weigh_in.at[d], os_.at[0], or_.at[0], along_z(d))

    def all_weigh():
        return remote(weigh.at[pl.ds(1, 7)], weigh_in.at[pl.ds(1, 7)], os_.at[0], or_.at[0], partner)

    weigh_in[0] = weigh[0]

    lanes = lax.broadcasted_iota(jnp.int32, (8, HEAD), 1).astype(F32)
    loads[3].wait()

    def group(d, last):
        for dy in range(4):
            if d + dy > 0:
                core_arrival(d, dy).wait_recv()

        def score(h, side):
            q = query[:, pl.ds(pl.multiple_of(h * HEAD, HEAD), HEAD)]
            top = None
            for dy in range(4):
                ids = kv[0, d, dy, 256:272, :].astype(F32) * 128.0
                got = lax.dot_general(
                    q, kv[0, d, dy, 0:256, :], (((1,), (1,)), ((), ())), preferred_element_type=F32
                )
                left = jnp.where((ids[0:8] + lanes)[0:1] <= qpos[...], got[:, :HEAD], NEG)
                right = jnp.where((ids[8:16] + lanes)[0:1] <= qpos[...], got[:, HEAD:], NEG)
                scores[side, dy, :, 0:HEAD] = left
                scores[side, dy, :, HEAD:256] = right
                both = jnp.maximum(left, right)
                top = both if top is None else jnp.maximum(top, both)
            return jnp.broadcast_to(jnp.max(top, axis=1, keepdims=True), (256, HEAD))

        def gather(h, side, now):
            cols = pl.ds(pl.multiple_of(h * HEAD, HEAD), HEAD)
            if d > 0:
                old = peak[h]
                now = jnp.maximum(now, old)
                shrink = jnp.exp2((old - now) * SCALE2)
                sums = total[h] * shrink
                out = acc[h] * shrink
            else:
                sums = jnp.zeros((256, HEAD), F32)
                out = jnp.zeros((256, HEAD), F32)
            peak[h] = now
            for dy in range(4):
                left = jnp.exp2((scores[side, dy, :, 0:HEAD] - now) * SCALE2)
                right = jnp.exp2((scores[side, dy, :, HEAD:256] - now) * SCALE2)
                both = jnp.concatenate([left.astype(BF), right.astype(BF)], axis=1)
                out = out + jnp.dot(both, kv[1, d, dy, 0:256, :], preferred_element_type=F32)
                sums = sums + (left + right)
            if last:
                att[0, :, cols] = (out / jnp.sum(sums, axis=1, keepdims=True)).astype(BF)
                for dy in (1, 3, 2):
                    remote(att.at[0, :, cols], att.at[dy, :, cols], as_.at[dy - 1], ar.at[dy - 1], along_y(dy)).start()
            else:
                total[h] = sums
                acc[h] = out

        def two_heads(i, _):
            even = score(2 * i, 0)
            odd = score(2 * i + 1, 1)
            gather(2 * i, 0, even)
            gather(2 * i + 1, 1, odd)
            return 0

        lax.fori_loop(0, 2, two_heads, 0)

    for d in range(4):
        for dy in (1, 2, 3):
            y_copy(d, dy).wait_recv()
            core_copy(d, dy).start()
        if d > 0:
            if d == 1 or d == 3:
                proj_arrival(d // 2)
                proj_send(d // 2 + 1)
            group(d - 1, False)
    group(3, True)
    for d in range(1, 8):
        weigh_copy(d).start()

    def att_copy(dy):
        return remote(att.at[0], att.at[dy], as_.at[dy - 1], ar.at[dy - 1], along_y(dy))

    def core_part(dy):
        return remote(part.at[dy, 1 - core], other.at[dy], d1s.at[dy], d1r.at[dy], partner)

    def x_copy(dy, dx):
        i = dy * 3 + dx - 1
        return remote(send_x.at[dy, dx], from_x.at[dy, dx - 1], d2s.at[i], d2r.at[i], along_x(dx))

    def yz_copy(dy, dz):
        i = dy * 2 + dz
        return remote(send_z.at[dy, dz], from_z.at[dy, dz], d3s.at[i], d3r.at[i], along_yz(dy, dz))

    def project(dy):
        if dy > 0:
            att_copy(dy).wait_recv()
        for b in range(4):
            got = jnp.dot(att[dy], proj[b], preferred_element_type=F32)
            got = got.astype(BF).reshape(2, 4, 2, ROWS, 256)
            part[dy, 0, :, :, :, b * 256 : b * 256 + 256] = got[:, :, 0]
            part[dy, 1, :, :, :, b * 256 : b * 256 + 256] = got[:, :, 1]
        core_part(dy).start()

    def sum_cores(dy):
        core_part(dy).wait_recv()
        for dx in (2, 1, 3, 0):
            xt = (x + dx) % 4
            for dz in range(2):
                zt = (z_hi + dz) % 2
                mine = part[dy, core, zt, xt].astype(F32) + other[dy, zt, xt].astype(F32)
                send_x[dy, dx, dz] = mine.astype(BF)
            if dx > 0:
                x_copy(dy, dx).start()

    def sum_x(dy):
        for dx in (1, 2, 3):
            x_copy(dy, dx).wait_recv()
        for dz in (1, 0):
            got = send_x[dy, 0, dz].astype(F32) + from_x[dy, 0, dz].astype(F32)
            got = got + (from_x[dy, 1, dz].astype(F32) + from_x[dy, 2, dz].astype(F32))
            if dy + dz > 0:
                send_z[dy, dz] = got.astype(BF)
                yz_copy(dy, dz).start()
            else:
                from_z[0, 0] = got.astype(BF)

    def token_copy(dy, slot, step):
        to = (slot + step) % 8
        return remote(
            tok.at[dy, slot], tok.at[dy, to], ts.at[dy * 8 + to], tr.at[dy * 8 + to], along_z(step)
        )

    def last_step(dy):
        return (3, 1) if dy == 1 else (5, 7)

    def token_moves(dy):
        if dy in (0, 2):
            return [[(0, d) for d in (4, 3, 5, 2, 6, 1, 7)]]
        return [[(0, 1), (0, 7)], [(1, 1), (7, 7)], [(2, 1), (6, 7)], [last_step(dy)]]

    def forward(dy, hop):
        for slot, step in token_moves(dy)[hop - 1]:
            if hop > 1:
                token_copy(dy, (slot - step) % 8, step).wait_recv()
            token_copy(dy, slot, step).start()

    def sum_all(dy, square):
        for dz in range(2):
            if dy + dz > 0:
                yz_copy(dy, dz).wait_recv()
        from_y = (y + dy) % 4
        for b in range(4):
            cols = tile(b * 4 + from_y)
            near = slice(b * 256, b * 256 + 256)
            got = from_z[dy, 0, :, near].astype(F32) + from_z[dy, 1, :, near].astype(F32)
            state = (resid[:, cols].astype(F32) + got).astype(BF)
            hidden[:, cols] = state
            state = state.astype(F32)
            square = square + state * state
            tok[dy, 0, :, near] = (state * gain[:, cols]).astype(BF)
        forward(dy, 1)
        return square

    def all_rows(c):
        return remote(packed.at[c], rows.at[c, pl.ds(1, 15)], xs.at[c], xr.at[c], partner)

    def pack(dy):
        if dy in (0, 2):
            arriving = token_moves(dy)[0]
        else:
            arriving = [last_step(dy), token_moves(dy)[2][1 if dy == 1 else 0]]
        for slot, step in arriving:
            token_copy(dy, slot, step).wait_recv()

        def one(s, _):
            c = dy * SUB + s

            def columns(n, _):
                got = tok[dy, :, :, tile(s * (CW // 256) + n)].reshape(128, 256)
                got = jnp.dot(choose[...], got, preferred_element_type=F32)
                got = got.astype(BF).reshape(16, SLOT, 256)
                rows[c, 0, :, tile(n)] = got[0]
                packed[c, :, :, tile(n)] = got[1:]
                return 0

            lax.fori_loop(0, CW // 256, columns, 0)

            for i in FAR_FIRST:
                remote(packed.at[c, i - 1], rows.at[c, i], xs.at[c], xr.at[c], in_plane(i)).start()
            return 0

        lax.fori_loop(0, SUB, one, 0)

    def scale_copy(d):
        return remote(scale.at[0], scale.at[d], ss.at[0], sr.at[0], along_z(d))

    def all_scales():
        return remote(scale.at[pl.ds(1, 7)], scale.at[pl.ds(1, 7)], ss.at[0], sr.at[0], partner)

    def all_slot_scales():
        return remote(scale_out, scale_in.at[pl.ds(1, 15)], ss.at[1], sr.at[1], partner)

    loads[5].wait()
    loads[6].wait()
    loads[7].wait()
    proj_arrival(2)
    square = jnp.zeros((ROWS, 256), F32)
    project(0)

    all_weigh().wait_recv()
    slots = jnp.dot(perm[...], weigh_in[...].reshape(SLOTS, 128), preferred_element_type=F32)
    choose[...] = jnp.where(slots > 0.0, 1.0, 0.0).astype(BF)
    spread[...] = slots.T.astype(BF)

    sum_cores(0)
    project(1)
    sum_cores(1)
    project(3)
    start_far(0)
    sum_x(0)
    sum_cores(3)
    project(2)
    start_far(1)
    sum_x(1)
    sum_cores(2)
    square = sum_all(0, square)
    start_far(2)
    sum_x(3)
    square = sum_all(1, square)
    start_far(3)
    forward(1, 2)
    sum_x(2)
    pack(0)
    square = sum_all(3, square)
    forward(1, 3)
    forward(3, 2)
    forward(1, 4)
    square = sum_all(2, square)
    far_d.start()
    mean = jnp.sum(square, axis=1, keepdims=True) * (1.0 / D)
    factor = jnp.broadcast_to(lax.rsqrt(mean + EPS), (ROWS, 128))
    coarse = factor.astype(BF)
    fine = (factor - coarse.astype(F32)).astype(BF)
    lane = lax.broadcasted_iota(jnp.int32, (ROWS, 128), 1)
    scale[0] = jnp.where(lane < 64, coarse.astype(F32), fine.astype(F32)).astype(BF)
    for d in range(1, 8):
        scale_copy(d).start()
    forward(3, 3)
    pack(1)
    forward(3, 4)
    pack(3)
    pack(2)

    all_scales().wait_recv()
    got = jnp.dot(choose[...], scale[...].reshape(128, 128), preferred_element_type=F32)
    got = got.astype(BF).reshape(16, SLOT, 128)
    scale_in[0] = got[0]
    scale_out[...] = got[1:]

    for i in range(1, 16):
        remote(scale_out.at[i - 1], scale_in.at[i], ss.at[1], sr.at[1], in_plane(i)).start()

    acc_g[...] = jnp.zeros_like(acc_g)
    acc_u[...] = jnp.zeros_like(acc_u)

    for f in range(4):
        for c in local_weights(f):
            c.wait()
        for c in far_weights(f):
            c.wait_recv()

    def upward(s, dy):
        c = dy * SUB + s
        all_rows(c).wait_recv()

        def one(q, _):
            f = (y + 4 - q + dy) % 4
            got = rows[c, pl.ds(q * 4, 4)].reshape(4 * SLOT, CW)
            at = pl.ds(pl.multiple_of(q * 4 * SLOT, 4 * SLOT), 4 * SLOT)
            depth = pl.ds(s * 2, 2)
            for n in range(3):
                cols = slice(n * 256, n * 256 + 256)
                acc_g[at, cols] += jnp.dot(got, wg[f, depth, :, cols].reshape(CW, 256), preferred_element_type=F32)
                acc_u[at, cols] += jnp.dot(got, wu[f, depth, :, cols].reshape(CW, 256), preferred_element_type=F32)
            return 0

        lax.fori_loop(0, 4, one, 0)
        return dy

    for dy in (0, 1, 3, 2):
        lax.fori_loop(0, SUB, upward, dy)
    all_slot_scales().wait_recv()
    both = scale_in[...].reshape(SLOTS, 128).astype(F32)
    factor = both[:, 0:1] + both[:, 64:65]

    def activate(n, _):
        act[:, tile(n)] = (jax.nn.silu(acc_g[:, tile(n)] * factor) * (acc_u[:, tile(n)] * factor)).astype(BF)
        return 0

    lax.fori_loop(0, 3, activate, 0)
    local_d.wait()
    far_d.wait_recv()

    def all_back(c):
        return remote(back.at[c], ret.at[c, pl.ds(1, 15)], rs.at[c], rr.at[c], partner)

    def all_sums(c):
        return remote(summed.at[c, pl.ds(1, 7)], sums_in.at[c, pl.ds(1, 7)], fs.at[c], fr.at[c], partner)

    def downward(c, _):
        def columns(n, _):
            got = jnp.dot(act[...], wd[:, tile(c * (CW // 256) + n)], preferred_element_type=F32)
            got = got.astype(BF).reshape(16, SLOT, 256)
            ret[c, 0, :, tile(n)] = got[0]
            back[c, :, :, tile(n)] = got[1:]
            return 0

        lax.fori_loop(0, CW // 256, columns, 0)

        for i in FAR_FIRST:
            remote(back.at[c, i - 1], ret.at[c, i], rs.at[c], rr.at[c], plane_back(i)).start()
        return 0

    lax.fori_loop(0, NC, downward, 0)

    for d in (1, 2, 3):
        z_copy(d).wait_send()
        proj_sent(d - 1)
        att_copy(d).wait_send()
    for d in range(4):
        for dy in (1, 2, 3):
            y_copy(d, dy).wait_send()
        for dy in range(4):
            if d + dy > 0:
                core_copy(d, dy).wait_send()
    for dy in range(4):
        core_part(dy).wait_send()
        for dx in (1, 2, 3):
            x_copy(dy, dx).wait_send()
        for dz in range(2):
            if dy + dz > 0:
                yz_copy(dy, dz).wait_send()
        for moves in token_moves(dy):
            for slot, step in moves:
                token_copy(dy, slot, step).wait_send()
        for c in far_weights(dy):
            c.wait_send()
    all_weigh().wait_send()
    all_scales().wait_send()
    all_slot_scales().wait_send()

    def drain_rows(c, _):
        all_rows(c).wait_send()
        return 0

    lax.fori_loop(0, NC, drain_rows, 0)
    far_d.wait_send()

    def combine(c, _):
        all_back(c).wait_recv()

        def columns(n, _):
            got = ret[c, :, :, tile(n)].reshape(SLOTS, 256)
            got = jnp.dot(spread[...], got, preferred_element_type=F32)
            summed[c, :, :, tile(n)] = got.astype(BF).reshape(8, ROWS, 256)
            return 0

        lax.fori_loop(0, CW // 256, columns, 0)

        for d in (4, 3, 5, 2, 6, 1, 7):
            remote(summed.at[c, d], sums_in.at[c, d], fs.at[c], fr.at[c], along_z(8 - d)).start()
        return 0

    lax.fori_loop(0, NC, combine, 0)

    def finish(c, _):
        all_sums(c).wait_recv()
        got = summed[c, 0].astype(F32)
        for d in range(1, 8):
            got = got + sums_in[c, d].astype(F32)
        out_ref[:, chunk(c)] = (hidden[:, chunk(c)].astype(F32) + got).astype(BF)
        return 0

    lax.fori_loop(0, NC, finish, 0)

    def drain(c, _):
        all_back(c).wait_send()
        all_sums(c).wait_send()
        return 0

    lax.fori_loop(0, NC, drain, 0)


def slot_order():
    perm = np.zeros((SLOTS, SLOTS), np.float32)
    for p in range(16):
        for s in range(8):
            for r in range(CAP):
                perm[p * SLOT + s * CAP + r, s * 16 * CAP + r * 16 + p] = 1.0
    return perm


VMEM = pl.BlockSpec(memory_space=pltpu.VMEM)
SMEM = pl.BlockSpec(memory_space=pltpu.SMEM)
ANY = pl.BlockSpec(memory_space=pl.ANY)
SHAPE = jax.ShapeDtypeStruct
DMA = pltpu.SemaphoreType.DMA


def both_ways(*counts):
    return [DMA((n,)) for n in counts for _ in range(2)]


def layer(*operands):
    return pl.pallas_call(
        layer_kernel,
        out_shape=SHAPE((ROWS, D), BF),
        in_specs=[SMEM] + [ANY] * 12,
        out_specs=VMEM,
        scratch_shapes=[
            pltpu.VMEM((256, 512), BF),
            pltpu.VMEM((ROWS, D), BF),
            pltpu.VMEM((1, D), F32),
            pltpu.VMEM((TOP, ROWS), jnp.int32),
            pltpu.VMEM((TOP, ROWS), F32),
            pltpu.VMEM((SLOTS, SLOTS), BF),
            pltpu.VMEM((2, 4, 4, 272, HEAD), BF),
            pltpu.VMEM((2, 4, 256, 256), F32),
            pltpu.VMEM((256, HEAD), F32),
            pltpu.VMEM((4, 256, HEAD), F32),
            pltpu.VMEM((4, 256, HEAD), F32),
            pltpu.VMEM((4, 256, HEAD), F32),
            pltpu.VMEM((4, 256, 512), BF),
            pltpu.VMEM((4, 512, 256), BF),
            pltpu.VMEM((4, 2, 2, 4, ROWS, 1024), BF),
            pltpu.VMEM((4, 2, 4, ROWS, 1024), BF),
            pltpu.VMEM((4, 4, 2, ROWS, 1024), BF),
            pltpu.VMEM((4, 3, 2, ROWS, 1024), BF),
            pltpu.VMEM((4, 2, ROWS, 1024), BF),
            pltpu.VMEM((4, 2, ROWS, 1024), BF),
            pltpu.VMEM((ROWS, D), BF),
            pltpu.VMEM((4, 4, 256, 2 * FH), BF),
            pltpu.VMEM((4, 4, 256, 2 * FH), BF),
            pltpu.VMEM((2 * FH, D), BF),
            pltpu.VMEM((8, CAP, 16, 128), BF),
            pltpu.VMEM((8, CAP, 16, 128), BF),
            pltpu.VMEM((SLOTS, 128), BF),
            pltpu.VMEM((128, SLOTS), BF),
            pltpu.VMEM((4, 8, ROWS, 1024), BF),
            pltpu.VMEM((8, ROWS, 128), BF),
            pltpu.VMEM((NC, 15, SLOT, CW), BF),
            pltpu.VMEM((NC, 16, SLOT, CW), BF),
            pltpu.VMEM((15, SLOT, 128), BF),
            pltpu.VMEM((16, SLOT, 128), BF),
            pltpu.VMEM((SLOTS, 2 * FH), F32),
            pltpu.VMEM((SLOTS, 2 * FH), F32),
            pltpu.VMEM((SLOTS, 2 * FH), BF),
            pltpu.VMEM((NC, 15, SLOT, CW), BF),
            pltpu.VMEM((NC, 16, SLOT, CW), BF),
            pltpu.VMEM((NC, 8, ROWS, CW), BF),
            pltpu.VMEM((NC, 8, ROWS, CW), BF),
            DMA((9,)),
            *both_ways(3, 12, 16, 3, 3, 3, 4, 12, 8),
            DMA((4,)), DMA((4,)), DMA((1,)),
            *both_ways(4, 4, 1, 1, 32, 2, NC, NC, NC),
        ],
        compiler_params=pltpu.CompilerParams(
            collective_id=0, has_side_effects=True, vmem_limit_bytes=60 * 1024 * 1024
        ),
        name="layer",
    )(*operands)


def local(
    queries,
    key_states,
    value_head_states,
    block_order,
    out_proj,
    residual,
    norm_gain,
    w_gate,
    w_up,
    w_down,
    routes,
    gate_weights,
):
    perm = jnp.asarray(slot_order(), BF)
    return layer(
        block_order, queries, key_states, value_head_states, out_proj, residual,
        norm_gain.reshape(1, D), routes.T, gate_weights.T, perm,
        w_gate.reshape(4, 4, 256, FH), w_up.reshape(4, 4, 256, FH), w_down,
    )


def solution(mesh):
    return jax.shard_map(
        local,
        mesh=mesh,
        in_specs=(
            P("ctx", "ep"),
            P("ctx", None),
            P("ctx", None),
            P("ctx"),
            P("ep", "ctx"),
            P(("ctx", "ep"), None),
            P(),
            P(None, ("ctx", "ep")),
            P(None, ("ctx", "ep")),
            P(("ctx", "ep"), None),
            P(("ctx", "ep"), None),
            P(("ctx", "ep"), None),
        ),
        out_specs=P(("ctx", "ep"), None),
        check_vma=False,
    )
```

```python
import math

import jax
import jax.numpy as jnp
import numpy as np
from jax import lax
from jax.experimental import pallas as pl
from jax.experimental.pallas import tpu as pltpu
from jax.sharding import PartitionSpec as P

MESH = pl.DeviceIdType.MESH
BF = jnp.bfloat16
F32 = jnp.float32

D = 4096
HEAD = 128
TOP = 8
NEG = -1e30
EPS = 1e-06
SCALE2 = math.log2(math.e) / math.sqrt(HEAD)

SUB = 2
NC = 4 * SUB
CW = D // NC
ROWS = 16
CAP = 3
SLOT = 8 * CAP
SLOTS = 16 * SLOT
FH = 384
FAR_FIRST = sorted(range(1, 16), key=lambda i: -(min(i // 4, 4 - i // 4) + min(i % 4, 4 - i % 4)))


def here():
    c = lax.axis_index("ctx")
    e = lax.axis_index("ep")
    return (e // 2) % 4, c % 4, e // 8, c // 4, e % 2


def device(x, y, z_hi, z_lo, core):
    return (z_lo * 4 + y, z_hi * 8 + x * 2 + core)


def remote(src, dst, send, recv, target):
    return pltpu.make_async_remote_copy(
        src_ref=src, dst_ref=dst, send_sem=send, recv_sem=recv, device_id=target, device_id_type=MESH
    )


def layer_kernel(
    order_ref, q_hbm, k_hbm, v_hbm, proj_hbm, resid_hbm, gain_hbm, routes_hbm, gates_hbm, perm_hbm, wg_hbm, wu_hbm, wd_hbm,
    out_ref,
    query, resid, gain, routes, gates, perm,
    kv, scores, qpos, peak, total, acc, att, proj, part, other, send_x, from_x, send_z, from_z, hidden,
    wg, wu, wd, weigh, weigh_in, choose, spread,
    tok, scale, packed, rows, scale_out, scale_in, acc_g, acc_u, act, back, ret, summed, sums_in,
    load_sem, zs, zr, ys, yr, cs, cr, rights, rightr, lefts, leftr, as_, ar, d1s, d1r, d2s, d2r, d3s, d3r,
    lg, lu, ld, gs, gr, us, ur, ws, wr, os_, or_, ts, tr, ss, sr, xs, xr, rs, rr, fs, fr,
):
    x, y, z_hi, z_lo, core = here()
    z = z_hi * 4 + z_lo
    partner = device(x, y, z_hi, z_lo, 1 - core)

    def ahead(at, d, size):
        return lax.rem(at + d, size) if d else at

    ctx_at = [z_lo * 4 + ahead(y, d, 4) for d in range(4)]
    ep_at = [z_hi * 8 + ahead(x, d, 4) * 2 + core for d in range(4)]
    spans = [(ahead(z_lo, d, 4) * 4 + y, ep_at[0]) for d in range(4)]
    across = (1 - z_hi) * 8 + x * 2 + core
    columns_at = [
        (lax.rem(ahead(z, d, 8), 4) * 4 + y, (ahead(z, d, 8) // 4) * 8 + x * 2 + core) for d in range(8)
    ]

    def in_span(d):
        return spans[d]

    def along_y(d):
        return (ctx_at[d], ep_at[0])

    def along_x(d):
        return (ctx_at[0], ep_at[d])

    def along_yz(dy, dz):
        return (ctx_at[(4 - dy) % 4], across if dz else ep_at[0])

    def along_z(d):
        return columns_at[d % 8]

    def in_plane(i):
        return (ctx_at[i // 4], ep_at[i % 4])

    def plane_back(i):
        return (ctx_at[(4 - i // 4) % 4], ep_at[(4 - i % 4) % 4])

    def chunk(c):
        return pl.ds(pl.multiple_of(c * CW, CW), CW)

    def tile(n):
        return pl.ds(pl.multiple_of(n * 256, 256), 256)

    head_col = pl.multiple_of((z_hi * 2 + x // 2) * HEAD, HEAD)
    loads = [
        pltpu.make_async_copy(src, dst, load_sem.at[i])
        for i, (src, dst) in enumerate([
            (k_hbm.at[:, pl.ds(head_col, HEAD)], kv.at[0, 0, 0, pl.ds(0, 256), :]),
            (v_hbm.at[:, pl.ds(head_col, HEAD)], kv.at[1, 0, 0, pl.ds(0, 256), :]),
            (proj_hbm, proj.at[z_lo]),
            (q_hbm, query),
            (routes_hbm, routes),
            (perm_hbm, perm),
            (resid_hbm, resid),
            (gain_hbm, gain),
            (gates_hbm, gates),
        ])
    ]
    for c in loads:
        c.start()

    barrier = pltpu.get_barrier_semaphore()

    def greet(target):
        pl.semaphore_signal(barrier, inc=1, device_id=target, device_id_type=MESH)

    greet(partner)
    for d in range(1, 8):
        greet(along_z(d))
    for i in range(1, 16):
        greet(in_plane(i))
    for dy in (1, 2, 3):
        greet(along_yz(dy, 1))

    first = order_ref[0].astype(F32)
    second = order_ref[1].astype(F32)
    row16 = lax.broadcasted_iota(jnp.int32, (16, HEAD), 0)
    tail = jnp.where(row16 < 8, first, second).astype(BF)
    kv[0, 0, 0, 256:272, :] = tail
    kv[1, 0, 0, 256:272, :] = tail
    row = lax.broadcasted_iota(jnp.int32, (256, HEAD), 0)
    qpos[...] = jnp.where(row < 128, first * 128.0 + row.astype(F32), (second - 1.0) * 128.0 + row.astype(F32))

    loads[0].wait()
    loads[1].wait()
    own_half = pl.ds(0, FH)
    far_half = pl.ds(FH, FH)

    def local_weights(f):
        return (
            pltpu.make_async_copy(wg_hbm.at[:, f], wg.at[f, :, :, own_half], lg.at[f]),
            pltpu.make_async_copy(wu_hbm.at[:, f], wu.at[f, :, :, own_half], lu.at[f]),
        )

    def far_weights(f):
        return (
            remote(wg_hbm.at[:, f], wg.at[f, :, :, far_half], gs.at[f], gr.at[f], partner),
            remote(wu_hbm.at[:, f], wu.at[f, :, :, far_half], us.at[f], ur.at[f], partner),
        )

    local_d = pltpu.make_async_copy(wd_hbm, wd.at[own_half, :], ld.at[0])
    far_d = remote(wd_hbm, wd.at[far_half, :], ws.at[0], wr.at[0], partner)

    def start_far(f):
        for c in far_weights(f):
            c.start()

    for f in range(4):
        for c in local_weights(f):
            c.start()
    local_d.start()

    pl.semaphore_wait(barrier, 26)

    def z_copy(d):
        return remote(kv.at[core, 0, 0], kv.at[core, d, 0], zs.at[d - 1], zr.at[d - 1], in_span(d))

    def y_copy(d, dy):
        i = d * 3 + dy - 1
        return remote(kv.at[core, d, 0], kv.at[core, d, dy], ys.at[i], yr.at[i], along_y(dy))

    def core_copy(d, dy):
        i = d * 4 + dy
        return remote(kv.at[core, d, dy], kv.at[core, d, dy], cs.at[i], cr.at[i], partner)

    def core_arrival(d, dy):
        i = d * 4 + dy
        return remote(kv.at[1 - core, d, dy], kv.at[1 - core, d, dy], cs.at[i], cr.at[i], partner)

    def right_copy(p, slot):
        return remote(proj.at[slot], proj.at[slot], rights.at[p], rightr.at[p], in_span(1))

    def left_copy(p, slot):
        return remote(proj.at[slot], proj.at[slot], lefts.at[p], leftr.at[p], in_span(3))

    def proj_send(p):
        @pl.when((z_lo <= 2) & (z_lo >= p))
        def _():
            right_copy(p, z_lo - p).start()

        @pl.when((z_lo >= 1) & (z_lo + p <= 3))
        def _():
            left_copy(p, z_lo + p).start()

    def proj_arrival(p):
        @pl.when(z_lo >= p + 1)
        def _():
            right_copy(p, z_lo - 1 - p).wait_recv()

        @pl.when(z_lo <= 2 - p)
        def _():
            left_copy(p, z_lo + 1 + p).wait_recv()

    def proj_sent(p):
        @pl.when((z_lo <= 2) & (z_lo >= p))
        def _():
            right_copy(p, z_lo - p).wait_send()

        @pl.when((z_lo >= 1) & (z_lo + p <= 3))
        def _():
            left_copy(p, z_lo + p).wait_send()

    for d in (1, 2, 3):
        z_copy(d).start()
    for dy in (1, 2, 3):
        y_copy(0, dy).start()

    loads[4].wait()
    loads[8].wait()
    token = lax.broadcasted_iota(jnp.int32, (ROWS, 128), 0)
    lane = lax.broadcasted_iota(jnp.int32, (ROWS, 128), 1)
    repeat = jnp.where((lane & 15) == token, 1.0, 0.0)
    named_by = jnp.dot(routes[...].astype(F32), repeat, preferred_element_type=F32)
    weight_by = jnp.dot(gates[...], repeat, preferred_element_type=F32)
    row = lax.broadcasted_iota(jnp.int32, (128, 128), 0)
    lane = lax.broadcasted_iota(jnp.int32, (128, 128), 1)
    z_to = (z + (row >> 4)) & 7
    x_to = (x + (row & 3)) & 3
    y_to = (y + ((row >> 2) & 3)) & 3
    expert = ((z_to & 3) * 32 + y_to * 8 + (z_to >> 2) * 4 + x_to).astype(F32)
    own = (lane >> 4) == (row >> 4)
    named = jnp.zeros((128, 128), F32)
    weight = jnp.zeros((128, 128), F32)
    for j in range(TOP):
        hit = jnp.where(own & (jnp.abs(named_by[j : j + 1, :] - expert) < 0.5), 1.0, 0.0)
        named = named + hit
        weight = weight + hit * weight_by[j : j + 1, :]
    before = jnp.where(row < lane, 1.0, 0.0).astype(BF)
    rank = jnp.dot(named.astype(BF), before, preferred_element_type=F32)
    for r in range(CAP):
        at = jnp.where((named > 0.5) & (jnp.abs(rank - r) < 0.5), 1.0, 0.0)
        weigh[:, r] = (at * weight).reshape(8, 16, 128).astype(BF)

    for d in (1, 2, 3):
        z_copy(d).wait_recv()
        if d == 3:
            loads[2].wait()
            proj_send(0)
        for dy in (1, 2, 3):
            y_copy(d, dy).start()
        core_copy(d, 0).start()
    def weigh_copy(d):
        return remote(weigh.at[d], weigh_in.at[d], os_.at[0], or_.at[0], along_z(d))

    def all_weigh():
        return remote(weigh.at[pl.ds(1, 7)], weigh_in.at[pl.ds(1, 7)], os_.at[0], or_.at[0], partner)

    weigh_in[0] = weigh[0]

    lanes = lax.broadcasted_iota(jnp.int32, (8, HEAD), 1).astype(F32)
    loads[3].wait()

    def group(d, last):
        for dy in range(4):
            if d + dy > 0:
                core_arrival(d, dy).wait_recv()

        def score(h, side):
            q = query[:, pl.ds(pl.multiple_of(h * HEAD, HEAD), HEAD)]
            top = None
            for dy in range(4):
                ids = kv[0, d, dy, 256:272, :].astype(F32) * 128.0
                got = lax.dot_general(
                    q, kv[0, d, dy, 0:256, :], (((1,), (1,)), ((), ())), preferred_element_type=F32
                )
                left = jnp.where((ids[0:8] + lanes)[0:1] <= qpos[...], got[:, :HEAD], NEG)
                right = jnp.where((ids[8:16] + lanes)[0:1] <= qpos[...], got[:, HEAD:], NEG)
                scores[side, dy, :, 0:HEAD] = left
                scores[side, dy, :, HEAD:256] = right
                both = jnp.maximum(left, right)
                top = both if top is None else jnp.maximum(top, both)
            return jnp.broadcast_to(jnp.max(top, axis=1, keepdims=True), (256, HEAD))

        def gather(h, side, now):
            cols = pl.ds(pl.multiple_of(h * HEAD, HEAD), HEAD)
            if d > 0:
                old = peak[h]
                now = jnp.maximum(now, old)
                shrink = jnp.exp2((old - now) * SCALE2)
                sums = total[h] * shrink
                out = acc[h] * shrink
            else:
                sums = jnp.zeros((256, HEAD), F32)
                out = jnp.zeros((256, HEAD), F32)
            peak[h] = now
            for dy in range(4):
                left = jnp.exp2((scores[side, dy, :, 0:HEAD] - now) * SCALE2)
                right = jnp.exp2((scores[side, dy, :, HEAD:256] - now) * SCALE2)
                both = jnp.concatenate([left.astype(BF), right.astype(BF)], axis=1)
                out = out + jnp.dot(both, kv[1, d, dy, 0:256, :], preferred_element_type=F32)
                sums = sums + (left + right)
            if last:
                att[0, :, cols] = (out / jnp.sum(sums, axis=1, keepdims=True)).astype(BF)
                for dy in (1, 3, 2):
                    remote(att.at[0, :, cols], att.at[dy, :, cols], as_.at[dy - 1], ar.at[dy - 1], along_y(dy)).start()
            else:
                total[h] = sums
                acc[h] = out

        def two_heads(i, _):
            even = score(2 * i, 0)
            odd = score(2 * i + 1, 1)
            gather(2 * i, 0, even)
            gather(2 * i + 1, 1, odd)
            return 0

        lax.fori_loop(0, 2, two_heads, 0)

    for d in range(4):
        for dy in (1, 2, 3):
            y_copy(d, dy).wait_recv()
            core_copy(d, dy).start()
        if d > 0:
            if d == 1 or d == 3:
                proj_arrival(d // 2)
                proj_send(d // 2 + 1)
            group(d - 1, False)
    group(3, True)
    for d in range(1, 8):
        weigh_copy(d).start()

    def att_copy(dy):
        return remote(att.at[0], att.at[dy], as_.at[dy - 1], ar.at[dy - 1], along_y(dy))

    def core_part(dy):
        return remote(part.at[dy, 1 - core], other.at[dy], d1s.at[dy], d1r.at[dy], partner)

    def x_copy(dy, dx):
        i = dy * 3 + dx - 1
        return remote(send_x.at[dy, dx], from_x.at[dy, dx - 1], d2s.at[i], d2r.at[i], along_x(dx))

    def yz_copy(dy, dz):
        i = dy * 2 + dz
        return remote(send_z.at[dy, dz], from_z.at[dy, dz], d3s.at[i], d3r.at[i], along_yz(dy, dz))

    def project(dy):
        if dy > 0:
            att_copy(dy).wait_recv()
        for b in range(4):
            got = jnp.dot(att[dy], proj[b], preferred_element_type=F32)
            got = got.astype(BF).reshape(2, 4, 2, ROWS, 256)
            part[dy, 0, :, :, :, b * 256 : b * 256 + 256] = got[:, :, 0]
            part[dy, 1, :, :, :, b * 256 : b * 256 + 256] = got[:, :, 1]
        core_part(dy).start()

    def sum_cores(dy):
        core_part(dy).wait_recv()
        for dx in (2, 1, 3, 0):
            xt = (x + dx) % 4
            for dz in range(2):
                zt = (z_hi + dz) % 2
                mine = part[dy, core, zt, xt].astype(F32) + other[dy, zt, xt].astype(F32)
                send_x[dy, dx, dz] = mine.astype(BF)
            if dx > 0:
                x_copy(dy, dx).start()

    def sum_x(dy):
        for dx in (1, 2, 3):
            x_copy(dy, dx).wait_recv()
        for dz in (1, 0):
            got = send_x[dy, 0, dz].astype(F32) + from_x[dy, 0, dz].astype(F32)
            got = got + (from_x[dy, 1, dz].astype(F32) + from_x[dy, 2, dz].astype(F32))
            if dy + dz > 0:
                send_z[dy, dz] = got.astype(BF)
                yz_copy(dy, dz).start()
            else:
                from_z[0, 0] = got.astype(BF)

    def token_copy(dy, slot, step):
        to = (slot + step) % 8
        return remote(
            tok.at[dy, slot], tok.at[dy, to], ts.at[dy * 8 + to], tr.at[dy * 8 + to], along_z(step)
        )

    def last_step(dy):
        return (3, 1) if dy == 1 else (5, 7)

    def token_moves(dy):
        if dy in (0, 2):
            return [[(0, d) for d in (4, 3, 5, 2, 6, 1, 7)]]
        return [[(0, 1), (0, 7)], [(1, 1), (7, 7)], [(2, 1), (6, 7)], [last_step(dy)]]

    def forward(dy, hop):
        for slot, step in token_moves(dy)[hop - 1]:
            if hop > 1:
                token_copy(dy, (slot - step) % 8, step).wait_recv()
            token_copy(dy, slot, step).start()

    def sum_all(dy, square):
        for dz in range(2):
            if dy + dz > 0:
                yz_copy(dy, dz).wait_recv()
        from_y = (y + dy) % 4
        for b in range(4):
            cols = tile(b * 4 + from_y)
            near = slice(b * 256, b * 256 + 256)
            got = from_z[dy, 0, :, near].astype(F32) + from_z[dy, 1, :, near].astype(F32)
            state = (resid[:, cols].astype(F32) + got).astype(BF)
            hidden[:, cols] = state
            state = state.astype(F32)
            square = square + state * state
            tok[dy, 0, :, near] = (state * gain[:, cols]).astype(BF)
        forward(dy, 1)
        return square

    def all_rows(c):
        return remote(packed.at[c], rows.at[c, pl.ds(1, 15)], xs.at[c], xr.at[c], partner)

    def pack(dy):
        if dy in (0, 2):
            arriving = token_moves(dy)[0]
        else:
            arriving = [last_step(dy), token_moves(dy)[2][1 if dy == 1 else 0]]
        for slot, step in arriving:
            token_copy(dy, slot, step).wait_recv()

        def one(s, _):
            c = dy * SUB + s

            def columns(n, _):
                got = tok[dy, :, :, tile(s * (CW // 256) + n)].reshape(128, 256)
                got = jnp.dot(choose[...], got, preferred_element_type=F32)
                got = got.astype(BF).reshape(16, SLOT, 256)
                rows[c, 0, :, tile(n)] = got[0]
                packed[c, :, :, tile(n)] = got[1:]
                return 0

            lax.fori_loop(0, CW // 256, columns, 0)

            for i in FAR_FIRST:
                remote(packed.at[c, i - 1], rows.at[c, i], xs.at[c], xr.at[c], in_plane(i)).start()
            return 0

        lax.fori_loop(0, SUB, one, 0)

    def scale_copy(d):
        return remote(scale.at[0], scale.at[d], ss.at[0], sr.at[0], along_z(d))

    def all_scales():
        return remote(scale.at[pl.ds(1, 7)], scale.at[pl.ds(1, 7)], ss.at[0], sr.at[0], partner)

    def all_slot_scales():
        return remote(scale_out, scale_in.at[pl.ds(1, 15)], ss.at[1], sr.at[1], partner)

    loads[5].wait()
    loads[6].wait()
    loads[7].wait()
    proj_arrival(2)
    square = jnp.zeros((ROWS, 256), F32)
    project(0)

    all_weigh().wait_recv()
    slots = jnp.dot(perm[...], weigh_in[...].reshape(SLOTS, 128), preferred_element_type=F32)
    choose[...] = jnp.where(slots > 0.0, 1.0, 0.0).astype(BF)
    spread[...] = slots.T.astype(BF)

    sum_cores(0)
    project(1)
    sum_cores(1)
    project(3)
    start_far(0)
    sum_x(0)
    sum_cores(3)
    project(2)
    start_far(1)
    sum_x(1)
    sum_cores(2)
    square = sum_all(0, square)
    start_far(2)
    sum_x(3)
    square = sum_all(1, square)
    start_far(3)
    forward(1, 2)
    sum_x(2)
    pack(0)
    square = sum_all(3, square)
    forward(1, 3)
    forward(3, 2)
    forward(1, 4)
    square = sum_all(2, square)
    far_d.start()
    mean = jnp.sum(square, axis=1, keepdims=True) * (1.0 / D)
    factor = jnp.broadcast_to(lax.rsqrt(mean + EPS), (ROWS, 128))
    coarse = factor.astype(BF)
    fine = (factor - coarse.astype(F32)).astype(BF)
    lane = lax.broadcasted_iota(jnp.int32, (ROWS, 128), 1)
    scale[0] = jnp.where(lane < 64, coarse.astype(F32), fine.astype(F32)).astype(BF)
    for d in range(1, 8):
        scale_copy(d).start()
    forward(3, 3)
    pack(1)
    forward(3, 4)
    pack(3)
    pack(2)

    all_scales().wait_recv()
    got = jnp.dot(choose[...], scale[...].reshape(128, 128), preferred_element_type=F32)
    got = got.astype(BF).reshape(16, SLOT, 128)
    scale_in[0] = got[0]
    scale_out[...] = got[1:]

    for i in range(1, 16):
        remote(scale_out.at[i - 1], scale_in.at[i], ss.at[1], sr.at[1], in_plane(i)).start()

    acc_g[...] = jnp.zeros_like(acc_g)
    acc_u[...] = jnp.zeros_like(acc_u)

    for f in range(4):
        for c in local_weights(f):
            c.wait()
        for c in far_weights(f):
            c.wait_recv()

    def upward(s, dy):
        c = dy * SUB + s
        all_rows(c).wait_recv()

        def one(q, _):
            f = (y + 4 - q + dy) % 4
            got = rows[c, pl.ds(q * 4, 4)].reshape(4 * SLOT, CW)
            at = pl.ds(pl.multiple_of(q * 4 * SLOT, 4 * SLOT), 4 * SLOT)
            depth = pl.ds(s * 2, 2)
            for n in range(3):
                cols = slice(n * 256, n * 256 + 256)
                acc_g[at, cols] += jnp.dot(got, wg[f, depth, :, cols].reshape(CW, 256), preferred_element_type=F32)
                acc_u[at, cols] += jnp.dot(got, wu[f, depth, :, cols].reshape(CW, 256), preferred_element_type=F32)
            return 0

        lax.fori_loop(0, 4, one, 0)
        return dy

    for dy in (0, 1, 3, 2):
        lax.fori_loop(0, SUB, upward, dy)
    all_slot_scales().wait_recv()
    both = scale_in[...].reshape(SLOTS, 128).astype(F32)
    factor = both[:, 0:1] + both[:, 64:65]

    def activate(n, _):
        act[:, tile(n)] = (jax.nn.silu(acc_g[:, tile(n)] * factor) * (acc_u[:, tile(n)] * factor)).astype(BF)
        return 0

    lax.fori_loop(0, 3, activate, 0)
    local_d.wait()
    far_d.wait_recv()

    def all_back(c):
        return remote(back.at[c], ret.at[c, pl.ds(1, 15)], rs.at[c], rr.at[c], partner)

    def all_sums(c):
        return remote(summed.at[c, pl.ds(1, 7)], sums_in.at[c, pl.ds(1, 7)], fs.at[c], fr.at[c], partner)

    def downward(c, _):
        def columns(n, _):
            got = jnp.dot(act[...], wd[:, tile(c * (CW // 256) + n)], preferred_element_type=F32)
            got = got.astype(BF).reshape(16, SLOT, 256)
            ret[c, 0, :, tile(n)] = got[0]
            back[c, :, :, tile(n)] = got[1:]
            return 0

        lax.fori_loop(0, CW // 256, columns, 0)

        for i in FAR_FIRST:
            remote(back.at[c, i - 1], ret.at[c, i], rs.at[c], rr.at[c], plane_back(i)).start()
        return 0

    lax.fori_loop(0, NC, downward, 0)

    for d in (1, 2, 3):
        z_copy(d).wait_send()
        proj_sent(d - 1)
        att_copy(d).wait_send()
    for d in range(4):
        for dy in (1, 2, 3):
            y_copy(d, dy).wait_send()
        for dy in range(4):
            if d + dy > 0:
                core_copy(d, dy).wait_send()
    for dy in range(4):
        core_part(dy).wait_send()
        for dx in (1, 2, 3):
            x_copy(dy, dx).wait_send()
        for dz in range(2):
            if dy + dz > 0:
                yz_copy(dy, dz).wait_send()
        for moves in token_moves(dy):
            for slot, step in moves:
                token_copy(dy, slot, step).wait_send()
        for c in far_weights(dy):
            c.wait_send()
    all_weigh().wait_send()
    all_scales().wait_send()
    all_slot_scales().wait_send()

    def drain_rows(c, _):
        all_rows(c).wait_send()
        return 0

    lax.fori_loop(0, NC, drain_rows, 0)
    far_d.wait_send()

    def combine(c, _):
        all_back(c).wait_recv()

        def columns(n, _):
            got = ret[c, :, :, tile(n)].reshape(SLOTS, 256)
            got = jnp.dot(spread[...], got, preferred_element_type=F32)
            summed[c, :, :, tile(n)] = got.astype(BF).reshape(8, ROWS, 256)
            return 0

        lax.fori_loop(0, CW // 256, columns, 0)

        for d in (4, 3, 5, 2, 6, 1, 7):
            remote(summed.at[c, d], sums_in.at[c, d], fs.at[c], fr.at[c], along_z(8 - d)).start()
        return 0

    lax.fori_loop(0, NC, combine, 0)

    def finish(c, _):
        all_sums(c).wait_recv()
        got = summed[c, 0].astype(F32)
        for d in range(1, 8):
            got = got + sums_in[c, d].astype(F32)
        out_ref[:, chunk(c)] = (hidden[:, chunk(c)].astype(F32) + got).astype(BF)
        return 0

    lax.fori_loop(0, NC, finish, 0)

    def drain(c, _):
        all_back(c).wait_send()
        all_sums(c).wait_send()
        return 0

    lax.fori_loop(0, NC, drain, 0)


def slot_order():
    perm = np.zeros((SLOTS, SLOTS), np.float32)
    for p in range(16):
        for s in range(8):
            for r in range(CAP):
                perm[p * SLOT + s * CAP + r, s * 16 * CAP + r * 16 + p] = 1.0
    return perm


VMEM = pl.BlockSpec(memory_space=pltpu.VMEM)
SMEM = pl.BlockSpec(memory_space=pltpu.SMEM)
ANY = pl.BlockSpec(memory_space=pl.ANY)
SHAPE = jax.ShapeDtypeStruct
DMA = pltpu.SemaphoreType.DMA


def both_ways(*counts):
    return [DMA((n,)) for n in counts for _ in range(2)]


def layer(*operands):
    return pl.pallas_call(
        layer_kernel,
        out_shape=SHAPE((ROWS, D), BF),
        in_specs=[SMEM] + [ANY] * 12,
        out_specs=VMEM,
        scratch_shapes=[
            pltpu.VMEM((256, 512), BF),
            pltpu.VMEM((ROWS, D), BF),
            pltpu.VMEM((1, D), F32),
            pltpu.VMEM((TOP, ROWS), jnp.int32),
            pltpu.VMEM((TOP, ROWS), F32),
            pltpu.VMEM((SLOTS, SLOTS), BF),
            pltpu.VMEM((2, 4, 4, 272, HEAD), BF),
            pltpu.VMEM((2, 4, 256, 256), F32),
            pltpu.VMEM((256, HEAD), F32),
            pltpu.VMEM((4, 256, HEAD), F32),
            pltpu.VMEM((4, 256, HEAD), F32),
            pltpu.VMEM((4, 256, HEAD), F32),
            pltpu.VMEM((4, 256, 512), BF),
            pltpu.VMEM((4, 512, 256), BF),
            pltpu.VMEM((4, 2, 2, 4, ROWS, 1024), BF),
            pltpu.VMEM((4, 2, 4, ROWS, 1024), BF),
            pltpu.VMEM((4, 4, 2, ROWS, 1024), BF),
            pltpu.VMEM((4, 3, 2, ROWS, 1024), BF),
            pltpu.VMEM((4, 2, ROWS, 1024), BF),
            pltpu.VMEM((4, 2, ROWS, 1024), BF),
            pltpu.VMEM((ROWS, D), BF),
            pltpu.VMEM((4, 4, 256, 2 * FH), BF),
            pltpu.VMEM((4, 4, 256, 2 * FH), BF),
            pltpu.VMEM((2 * FH, D), BF),
            pltpu.VMEM((8, CAP, 16, 128), BF),
            pltpu.VMEM((8, CAP, 16, 128), BF),
            pltpu.VMEM((SLOTS, 128), BF),
            pltpu.VMEM((128, SLOTS), BF),
            pltpu.VMEM((4, 8, ROWS, 1024), BF),
            pltpu.VMEM((8, ROWS, 128), BF),
            pltpu.VMEM((NC, 15, SLOT, CW), BF),
            pltpu.VMEM((NC, 16, SLOT, CW), BF),
            pltpu.VMEM((15, SLOT, 128), BF),
            pltpu.VMEM((16, SLOT, 128), BF),
            pltpu.VMEM((SLOTS, 2 * FH), F32),
            pltpu.VMEM((SLOTS, 2 * FH), F32),
            pltpu.VMEM((SLOTS, 2 * FH), BF),
            pltpu.VMEM((NC, 15, SLOT, CW), BF),
            pltpu.VMEM((NC, 16, SLOT, CW), BF),
            pltpu.VMEM((NC, 8, ROWS, CW), BF),
            pltpu.VMEM((NC, 8, ROWS, CW), BF),
            DMA((9,)),
            *both_ways(3, 12, 16, 3, 3, 3, 4, 12, 8),
            DMA((4,)), DMA((4,)), DMA((1,)),
            *both_ways(4, 4, 1, 1, 32, 2, NC, NC, NC),
        ],
        compiler_params=pltpu.CompilerParams(
            collective_id=0, has_side_effects=True, vmem_limit_bytes=60 * 1024 * 1024
        ),
        name="layer",
    )(*operands)


def local(
    queries,
    key_states,
    value_head_states,
    block_order,
    out_proj,
    residual,
    norm_gain,
    w_gate,
    w_up,
    w_down,
    routes,
    gate_weights,
):
    perm = jnp.asarray(slot_order(), BF)
    return layer(
        block_order, queries, key_states, value_head_states, out_proj, residual,
        norm_gain.reshape(1, D), routes.T, gate_weights.T, perm,
        w_gate.reshape(4, 4, 256, FH), w_up.reshape(4, 4, 256, FH), w_down,
    )


def solution(mesh):
    return jax.shard_map(
        local,
        mesh=mesh,
        in_specs=(
            P("ctx", "ep"),
            P("ctx", None),
            P("ctx", None),
            P("ctx"),
            P("ep", "ctx"),
            P(("ctx", "ep"), None),
            P(),
            P(None, ("ctx", "ep")),
            P(None, ("ctx", "ep")),
            P(("ctx", "ep"), None),
            P(("ctx", "ep"), None),
            P(("ctx", "ep"), None),
        ),
        out_specs=P(("ctx", "ep"), None),
        check_vma=False,
    )
```
